512 devices in a mesh: context: 32 (over z_lo, x, core), tensor: 16 (over y, z_hi).
Axes of the slice: x: 4, y: 4, z: 16 (z_hi: 4, z_lo: 4; z = z_hi * 4 + z_lo), core: 2. Of those that a mesh axis runs over, the one named last changes fastest.
Arguments:
- q_gate: bfloat16 [8192, 4096], P('tensor', 'context'), may hold values from -160 to 160
- k_gate: bfloat16 [8192, 4096], P('tensor', 'context'), may hold values from -6 to 6
- values: bfloat16 [8192, 4096], P('tensor', 'context'), may hold values from -6 to 6
- residues: float32 [8192, 16], P('tensor'), may hold values from -1.5 to 1.5
- rates: float32 [8192, 16], P('tensor'), may hold values from 3e-05 to 0.1
- gain: float32 [8192], P('tensor'), may hold values from 0.5 to 1.5
Outputs:
- normed: bfloat16 [8192, 4096], P('tensor', 'context')
The draws below stay inside these ranges and needn't reach their ends.
All inputs are finite; a program needn't handle non-finite values.
Results may differ from the reference program's by a relative error of at most 0.0057.
Values may be sent and summed in bfloat16 or wider, within the bound.
A program may use at most 64 MiB of HBM per device.

```python
import math
import jax
import jax.numpy as jnp
from jax import lax

C = 8192
MODES = 16
TOKENS = 4096


def draw_q_gate(key, part):
    key = jax.random.fold_in(key, 7)
    noise_key, channel_key, token_key = jax.random.split(key, 3)
    channel_ramp = jnp.arange(C, dtype=jnp.float32) / C
    noise_part = jnp.clip(jax.random.normal(noise_key, (C, TOKENS), jnp.float32), -4.0, 4.0)
    trend_part = jnp.exp(jnp.log(3.0) * channel_ramp)
    channel_scale = trend_part * jnp.exp(jnp.log(10.0) * jax.random.uniform(channel_key, (C,), jnp.float32))
    token_scale = jnp.exp(jnp.log(10.0) * jax.random.uniform(token_key, (TOKENS,), jnp.float32))
    return (noise_part * channel_scale[:, None] * token_scale[None, :] * 0.1).astype(jnp.bfloat16)


def level_of(own_key, shape, cuts, low, high):
    def one(position, shards_of):
        steps = jax.random.uniform(jax.random.fold_in(jax.random.fold_in(own_key, 6), position), (shards_of,), jnp.float32, low / len(cuts), high / len(cuts))
        return jnp.repeat(jnp.exp(steps), shape[position] // shards_of).reshape((-1,) + (1,) * (len(shape) - position - 1))

    factor_of = one(*cuts[0])
    for cut in cuts[1:]:
        factor_of = factor_of * one(*cut)
    return factor_of


def normal_values(key, extent, width, reach, cuts=(), kind=jnp.bfloat16):
    entries = width * jax.random.normal(key, extent, jnp.float32)
    if cuts:
        entries = entries * level_of(key, extent, cuts, -0.22, 0.18)
    return jnp.clip(entries, -reach, reach).astype(kind)


def setup_inputs(seed: int = 0) -> dict:
    key_list = jax.random.split(jax.random.key(seed), 7)
    return {
        "q_gate": draw_q_gate(jax.random.fold_in(key_list[6], 71), 0),
        "k_gate": normal_values(key_list[1], (C, TOKENS), 1.0, 6.0, ((0, 16), (1, 32))),
        "values": normal_values(key_list[2], (C, TOKENS), 1.0, 6.0, ((0, 16), (1, 32))),
        "residues": normal_values(key_list[3], (C, MODES), 0.35, 1.5, ((0, 16),), jnp.float32),
        "rates": jnp.clip(jnp.exp(math.log(0.1) - 8.111728 * jax.random.uniform(key_list[4], (C, MODES), jnp.float32) ** level_of(key_list[4], (C, MODES), ((0, 16),), -0.2, 0.2)), 2.9999999242136255e-05, 0.1),
        "gain": jnp.clip(1.0 + 0.1 * jax.random.normal(key_list[5], (C,), jnp.float32), 0.5, 1.5),
    }


def filter_taps(res_block, rate_block, steps_time):
    taps = jnp.zeros((res_block.shape[0], steps_time.shape[0]), jnp.float32)
    for index in range(MODES):
        rate_col = rate_block[:, index:index + 1]
        taps = taps + res_block[:, index:index + 1] * jnp.sqrt(rate_col) * jnp.exp(-rate_col * steps_time[None, :])
    return taps

def reference(q_gate, k_gate, values, residues, rates, gain):
    gated = (k_gate.astype(jnp.float32) * values.astype(jnp.float32)).astype(jnp.bfloat16)
    steps_time = jnp.arange(TOKENS).astype(jnp.float32)
    block = 256

    def mix_block(pieces):
        signal_part, res_part, rate_part = pieces
        taps = filter_taps(res_part, rate_part, steps_time)
        signal_spec = jnp.fft.rfft(signal_part.astype(jnp.float32), n=2 * TOKENS, axis=-1)
        filter_spec = jnp.fft.rfft(taps, n=2 * TOKENS, axis=-1)
        conv = jnp.fft.irfft(signal_spec * filter_spec, n=2 * TOKENS, axis=-1)[:, :TOKENS]
        return conv.astype(jnp.bfloat16)
    mixer = lax.map(mix_block, (gated.reshape(C // block, block, TOKENS), residues.reshape(C // block, block, MODES), rates.reshape(C // block, block, MODES))).reshape(C, TOKENS)
    gated_out = q_gate.astype(jnp.float32) * mixer.astype(jnp.float32)
    square_sum = lax.optimization_barrier(jnp.sum(gated_out * gated_out, axis=0))
    scale_row = lax.rsqrt(square_sum / C + 1e-05)
    return (gated_out * scale_row[None, :] * gain[:, None]).astype(jnp.bfloat16)
```

```python
import functools

import jax
import jax.numpy as jnp
from jax import lax
from jax.experimental import pallas as pl
from jax.experimental.pallas import tpu as pltpu
from jax.sharding import PartitionSpec as P

MESH = pl.DeviceIdType.MESH
CTX, TEN = "context", "tensor"
LANES = 128
SUB = 32
FIRST_OWNER = 8
OWNERS = 16
F32 = jnp.float32


def wait_bytes(ref, sem):
    pltpu.make_async_copy(ref, ref, sem).wait()


def kernel(
    n_ctx, n_ten, width,
    q_hbm, k_hbm, v_hbm, res_hbm, rate_hbm, gain_hbm,
    go_ref, scale_ref,
    q_v, k_v, v_v, res_v, rate_v, gain_v, go_t,
    g_pad, taps, powers, local, q_t, states, decays,
    s_buf, a_buf, r_buf, h_buf, h_in, t_buf,
    in_sem, ss1, rs1, ss2, rs2, ss3, rs3,
):
    me = lax.axis_index(CTX)
    ten = lax.axis_index(TEN)
    modes = rate_hbm.shape[0]
    chans, tokens = q_hbm.shape
    subs = tokens // SUB
    groups = chans // LANES
    rows = modes * groups // OWNERS
    per_tile = 8 // rows
    mine = lax.rem(me - FIRST_OWNER + n_ctx, n_ctx)
    is_owner = mine < OWNERS
    slot = lax.rem(mine, OWNERS)

    barrier = pltpu.get_barrier_semaphore()
    for step in range(1, n_ctx):
        pl.semaphore_signal(barrier, inc=1, device_id={CTX: lax.rem(me + step, n_ctx)}, device_id_type=MESH)
    for step in range(1, n_ten):
        pl.semaphore_signal(barrier, inc=1, device_id={TEN: lax.rem(ten + step, n_ten)}, device_id_type=MESH)

    loads = {}
    for place, (name, src, dst) in enumerate((
        ("rate", rate_hbm, rate_v), ("k", k_hbm, k_v), ("v", v_hbm, v_v),
        ("res", res_hbm, res_v), ("q", q_hbm, q_v), ("gain", gain_hbm, gain_v),
    )):
        loads[name] = pltpu.make_async_copy(src, dst, in_sem.at[place])
        loads[name].start()

    def tile(i, k):
        return pl.ds(8 * i, 8), pl.ds(LANES * k, LANES)

    g_pad[...] = jnp.zeros_like(g_pad)
    loads["rate"].wait()
    rate = rate_v[...]
    decay = jnp.exp(-rate)
    decay_sub = jnp.exp(-SUB * rate)
    loads["k"].wait()
    loads["v"].wait()
    gated = (k_v[...].astype(F32) * v_v[...].astype(F32)).astype(jnp.bfloat16).astype(F32)
    g_pad[:, 8:, :] = gated.T.reshape(subs, SUB, chans)

    def advance(i, hs):
        return tuple(decay * h + g_pad[s, pl.ds(8 + i, 1), :] for s, h in enumerate(hs))

    ends = lax.fori_loop(0, SUB, advance, (jnp.zeros((modes, chans), F32),) * subs, unroll=4)
    state = ends[0]
    states[0] = jnp.zeros((modes, chans), F32)
    for s in range(1, subs):
        states[s] = state
        state = decay_sub * state + ends[s]
    decay_all = jnp.exp(-float(tokens) * rate)
    for o in range(OWNERS):
        i, k, h = o // per_tile // groups, o // per_tile % groups, o % per_tile
        r, c = 8 * i + rows * h, LANES * k
        s_buf[o] = state[r : r + rows, c : c + LANES]
        a_buf[o] = decay_all[r : r + rows, c : c + LANES]

    pl.semaphore_wait(barrier, n_ctx - 1 + n_ten - 1)

    def give(o):
        pltpu.make_async_remote_copy(
            s_buf.at[o], r_buf.at[me], ss1, rs1, device_id={CTX: FIRST_OWNER + o}, device_id_type=MESH
        ).start()

    for step in range(1, OWNERS):
        give(lax.rem(slot + step, OWNERS))

    @pl.when(jnp.logical_not(is_owner))
    def _():
        give(slot)

    loads["res"].wait()
    weight = res_v[...] * jnp.sqrt(rate)
    ages = (lax.broadcasted_iota(jnp.int32, (SUB, chans), 0) + 1).astype(F32)
    total = jnp.zeros((SUB, chans), F32)
    for m in range(modes):
        power = weight[m : m + 1, :] * jnp.exp(-rate[m : m + 1, :] * ages)
        powers[m] = power
        total = total + power
    taps[7:8, :] = jnp.sum(weight, axis=0, keepdims=True)
    taps[8:, :] = total
    for s in range(subs):
        decays[s] = jnp.exp(-float(SUB * s) * rate)

    def convolve(k, carry):
        cols = pl.ds(pl.multiple_of(k * LANES, LANES), LANES)
        acc = [jnp.zeros((subs, 8, LANES), F32) for _ in range(SUB // 8)]
        for shift in range(8):
            pieces = [g_pad[:, pl.ds(8 + 8 * j - shift, 8), cols] for j in range(SUB // 8)]
            for b in range(SUB // 8):
                tap = taps[pl.ds(7 + 8 * b + shift, 1), cols]
                for j in range(b, SUB // 8):
                    acc[j] = acc[j] + tap * pieces[j - b]
        for j in range(SUB // 8):
            local[:, pl.ds(8 * j, 8), cols] = acc[j]
        return carry

    lax.fori_loop(0, groups, convolve, 0)

    @pl.when(is_owner)
    def _():
        r_buf[me] = s_buf[slot]
        wait_bytes(r_buf.at[pl.ds(0, n_ctx - 1)], rs1)
        ratio = a_buf[slot]
        held = jnp.zeros((rows, LANES), F32)
        for d in range(n_ctx):
            h_buf[d] = held
            if d < n_ctx - 1:
                held = ratio * held + r_buf[d]
        for step in range(1, n_ctx):
            d = lax.rem(me + step, n_ctx)
            pltpu.make_async_remote_copy(
                h_buf.at[d], h_in.at[slot], ss2, rs2, device_id={CTX: d}, device_id_type=MESH
            ).start()
        h_in[slot] = h_buf[me]

    loads["q"].wait()
    loads["gain"].wait()
    q_t[...] = q_v[...].astype(F32).T.reshape(subs, SUB, chans)

    @pl.when(is_owner)
    def _():
        wait_bytes(h_in.at[pl.ds(0, OWNERS - 1)], rs2)

    @pl.when(jnp.logical_not(is_owner))
    def _():
        wait_bytes(h_in, rs2)

    for o in range(OWNERS):
        i, k, h = o // per_tile // groups, o // per_tile % groups, o % per_tile
        r, c = pl.ds(8 * i + rows * h, rows), pl.ds(LANES * k, LANES)
        start = h_in[o]
        for s in range(subs):
            states[s, r, c] = states[s, r, c] + decays[s, r, c] * start

    square = jnp.zeros((subs, SUB, LANES), F32)
    for k in range(groups):
        cols = pl.ds(LANES * k, LANES)
        acc = local[:, :, cols]
        for m in range(modes):
            acc = acc + powers[m, :, cols][None] * states[:, pl.ds(m, 1), cols]
        out = q_t[:, :, cols] * acc.astype(jnp.bfloat16).astype(F32)
        square = square + out * out
        go_t[:, :, cols] = out * gain_v[:, cols]

    t_buf[ten] = jnp.sum(square.reshape(tokens, LANES).T, axis=0, keepdims=True)
    for step in range(1, n_ten):
        pltpu.make_async_remote_copy(
            t_buf.at[ten], t_buf.at[ten], ss3, rs3,
            device_id={TEN: lax.rem(ten + step, n_ten)}, device_id_type=MESH,
        ).start()

    go_ref[...] = go_t[...].reshape(tokens, chans).T

    @pl.when(is_owner)
    def _():
        wait_bytes(s_buf.at[pl.ds(0, OWNERS - 1)], ss1)
        wait_bytes(h_buf.at[pl.ds(0, n_ctx - 1)], ss2)

    @pl.when(jnp.logical_not(is_owner))
    def _():
        wait_bytes(s_buf, ss1)

    wait_bytes(t_buf.at[pl.ds(0, n_ten - 1)], ss3)
    wait_bytes(t_buf.at[pl.ds(0, n_ten - 1)], rs3)
    scale_ref[...] = lax.rsqrt(jnp.sum(t_buf[...], axis=0) / width + 1e-05)


def body(q_gate, k_gate, values, residues, rates, gain):
    n_ctx, n_ten = lax.axis_size(CTX), lax.axis_size(TEN)
    chans, tokens = q_gate.shape
    modes = rates.shape[1]
    subs, groups = tokens // SUB, chans // LANES
    rows = modes * groups // OWNERS
    vmem, dma = pltpu.VMEM, pltpu.SemaphoreType.DMA
    operands = (q_gate, k_gate, values, residues.T, rates.T, gain.reshape(1, chans))
    operands = [pltpu.with_memory_space_constraint(x, pltpu.HBM) for x in operands]
    gated_out, scale = pl.pallas_call(
        functools.partial(kernel, n_ctx, n_ten, float(chans * n_ten)),
        out_shape=(
            vmem((chans, tokens), F32),
            vmem((1, tokens), F32),
        ),
        in_specs=[pl.BlockSpec(memory_space=pltpu.HBM)] * 6,
        out_specs=(pl.BlockSpec(memory_space=pltpu.VMEM), pl.BlockSpec(memory_space=pltpu.VMEM)),
        scratch_shapes=[
            vmem((chans, tokens), jnp.bfloat16),
            vmem((chans, tokens), jnp.bfloat16),
            vmem((chans, tokens), jnp.bfloat16),
            vmem((modes, chans), F32),
            vmem((modes, chans), F32),
            vmem((1, chans), F32),
            vmem((subs, SUB, chans), F32),
            vmem((subs, 8 + SUB, chans), F32),
            vmem((8 + SUB, chans), F32),
            vmem((modes, SUB, chans), F32),
            vmem((subs, SUB, chans), F32),
            vmem((subs, SUB, chans), F32),
            vmem((subs, modes, chans), F32),
            vmem((subs, modes, chans), F32),
            vmem((OWNERS, rows, LANES), F32),
            vmem((OWNERS, rows, LANES), F32),
            vmem((n_ctx, rows, LANES), F32),
            vmem((n_ctx, rows, LANES), F32),
            vmem((OWNERS, rows, LANES), F32),
            vmem((n_ten, 1, tokens), F32),
            dma((6,)),
            dma(()), dma(()), dma(()), dma(()), dma(()), dma(()),
        ],
        compiler_params=pltpu.CompilerParams(
            collective_id=0, has_side_effects=True, vmem_limit_bytes=32 * 1024 * 1024
        ),
        name="hyena",
    )(*operands)
    return (gated_out * scale).astype(jnp.bfloat16)


def solution(mesh):
    return jax.shard_map(
        body,
        mesh=mesh,
        in_specs=(
            P(TEN, CTX),
            P(TEN, CTX),
            P(TEN, CTX),
            P(TEN, None),
            P(TEN, None),
            P(TEN),
        ),
        out_specs=P(TEN, CTX),
        check_vma=False,
    )
```

```python
import functools

import jax
import jax.numpy as jnp
from jax import lax
from jax.experimental import pallas as pl
from jax.experimental.pallas import tpu as pltpu
from jax.sharding import PartitionSpec as P

MESH = pl.DeviceIdType.MESH
CTX, TEN = "context", "tensor"
LANES = 128
SUB = 32
ROW = 8
LATER_DELEGATE = 1
WIDTH_DELEGATE = 5
F32 = jnp.float32


def wait_bytes(ref, sem):
    pltpu.make_async_copy(ref, ref, sem).wait()


def kernel(
    n_ctx, n_ten, width,
    q_hbm, k_hbm, v_hbm, res_hbm, rate_hbm, gain_hbm,
    go_ref, scale_ref,
    q_v, k_v, v_v, res_v, rate_v, gain_v, go_t,
    g_pad, taps, powers, local, q_t, states, decays,
    s_buf, a_buf, r_buf, p_out, p_in, c_out, c_in, t_buf,
    in_sem, ss1, rs1, ss2, rs2, ssc, rsc, ss3, rs3, row_in, later_in, width_in,
):
    me = lax.axis_index(CTX)
    ten = lax.axis_index(TEN)
    modes = rate_hbm.shape[0]
    chans, tokens = q_hbm.shape
    subs = tokens // SUB
    groups = chans // LANES
    tiles = modes // 8 * groups
    n_rows = n_ctx // ROW
    row, place = me // ROW, lax.rem(me, ROW)
    is_later_delegate = place == LATER_DELEGATE
    is_width_delegate = place == WIDTH_DELEGATE
    is_plain = jnp.logical_not(is_later_delegate | is_width_delegate)

    def signal(sem, **where):
        where = {{"ctx": CTX, "ten": TEN}[name]: at for name, at in where.items()}
        pl.semaphore_signal(sem, inc=1, device_id=where, device_id_type=MESH)

    barrier = pltpu.get_barrier_semaphore()
    for step in (4, 3, 5, 2, 6, 1, 7):
        other = lax.rem(place + step, ROW)

        @pl.when((other != LATER_DELEGATE) & (other != WIDTH_DELEGATE))
        def _():
            signal(barrier, ctx=row * ROW + other)

    def greet_earlier(r, carry):
        signal(barrier, ctx=r * ROW + LATER_DELEGATE)
        return carry

    lax.fori_loop(0, row, greet_earlier, 0)

    loads = {}
    for position, (name, src, dst) in enumerate((
        ("rate", rate_hbm, rate_v), ("k", k_hbm, k_v), ("v", v_hbm, v_v),
        ("res", res_hbm, res_v), ("q", q_hbm, q_v), ("gain", gain_hbm, gain_v),
    )):
        loads[name] = pltpu.make_async_copy(src, dst, in_sem.at[position])
        loads[name].start()

    g_pad[...] = jnp.zeros_like(g_pad)
    loads["rate"].wait()
    rate = rate_v[...]
    decay = jnp.exp(-rate)
    decay_sub = jnp.exp(-SUB * rate)
    loads["k"].wait()
    loads["v"].wait()
    gated = (k_v[...].astype(F32) * v_v[...].astype(F32)).astype(jnp.bfloat16).astype(F32)
    g_pad[:, 8:, :] = gated.T.reshape(subs, SUB, chans)

    def advance(i, hs):
        return tuple(decay * h + g_pad[s, pl.ds(8 + i, 1), :] for s, h in enumerate(hs))

    ends = lax.fori_loop(0, SUB, advance, (jnp.zeros((modes, chans), F32),) * subs, unroll=4)
    state = ends[0]
    states[0] = jnp.zeros((modes, chans), F32)
    for s in range(1, subs):
        states[s] = state
        state = decay_sub * state + ends[s]
    decay_all = jnp.exp(-float(tokens) * rate)

    def tile_of(j):
        return slice(8 * (j // groups), 8 * (j // groups) + 8), slice(LANES * (j % groups), LANES * (j % groups) + LANES)

    for j in range(tiles):
        s_buf[j] = state[tile_of(j)]
        a_buf[j] = decay_all[tile_of(j)]

    @pl.when(is_plain)
    def _():
        pl.semaphore_wait(barrier, ROW - 1)

    @pl.when((place ^ 1 == LATER_DELEGATE) | (place ^ 1 == WIDTH_DELEGATE))
    def _():
        signal(row_in, ctx=row * ROW + (place ^ 1))

    @pl.when(jnp.logical_not(is_plain))
    def _():
        pl.semaphore_wait(row_in, 1)

    for step in (4, 3, 5, 2, 6, 1, 7):
        other = lax.rem(place + step, ROW)
        pltpu.make_async_remote_copy(
            s_buf.at[other], r_buf.at[place], ss1, rs1, device_id={CTX: row * ROW + other}, device_id_type=MESH
        ).start()

    @pl.when(is_width_delegate)
    def _():
        for step in range(1, n_ten):
            signal(barrier, ten=lax.rem(ten + step, n_ten))

    @pl.when(is_later_delegate)
    def _():
        @pl.when(row < n_rows - 1)
        def _():
            pl.semaphore_wait(barrier, ROW * (n_rows - 1 - row))

        for step in (4, 3, 5, 2, 6, 1, 7):
            signal(later_in, ctx=row * ROW + lax.rem(place + step, ROW))

    loads["res"].wait()
    weight = res_v[...] * jnp.sqrt(rate)
    ages = (lax.broadcasted_iota(jnp.int32, (SUB, chans), 0) + 1).astype(F32)
    total = jnp.zeros((SUB, chans), F32)
    for m in range(modes):
        power = weight[m : m + 1, :] * jnp.exp(-rate[m : m + 1, :] * ages)
        powers[m] = power
        total = total + power
    taps[7:8, :] = jnp.sum(weight, axis=0, keepdims=True)
    taps[8:, :] = total
    for s in range(subs):
        decays[s] = jnp.exp(-float(SUB * s) * rate)

    r_buf[place] = s_buf[place]
    wait_bytes(r_buf.at[pl.ds(0, ROW - 1)], rs1)
    ratio = a_buf[place]
    held = jnp.zeros((8, LANES), F32)
    for d in range(ROW):
        p_out[d] = held
        held = ratio * held + r_buf[d]
    c_out[...] = held

    @pl.when(jnp.logical_not(is_later_delegate))
    def _():
        pl.semaphore_wait(later_in, 1)

    for later in range(n_rows - 1, 0, -1):
        @pl.when(later > row)
        def _():
            for step in (4, 3, 5, 2, 6, 1, 7, 0):
                pltpu.make_async_remote_copy(
                    c_out, c_in.at[row, place], ssc.at[later - 1], rsc.at[row],
                    device_id={CTX: later * ROW + lax.rem(place + step, ROW)}, device_id_type=MESH,
                ).start()

    for step in (4, 3, 5, 2, 6, 1, 7):
        other = lax.rem(place + step, ROW)
        pltpu.make_async_remote_copy(
            p_out.at[other], p_in.at[place], ss2, rs2, device_id={CTX: row * ROW + other}, device_id_type=MESH
        ).start()
    p_in[place] = p_out[place]

    def convolve(k, carry):
        cols = pl.ds(pl.multiple_of(k * LANES, LANES), LANES)
        acc = [jnp.zeros((subs, 8, LANES), F32) for _ in range(SUB // 8)]
        for shift in range(8):
            pieces = [g_pad[:, pl.ds(8 + 8 * j - shift, 8), cols] for j in range(SUB // 8)]
            for b in range(SUB // 8):
                tap = taps[pl.ds(7 + 8 * b + shift, 1), cols]
                for j in range(b, SUB // 8):
                    acc[j] = acc[j] + tap * pieces[j - b]
        for j in range(SUB // 8):
            local[:, pl.ds(8 * j, 8), cols] = acc[j]
        return carry

    lax.fori_loop(0, groups, convolve, 0)

    loads["q"].wait()
    loads["gain"].wait()
    q_t[...] = q_v[...].astype(F32).T.reshape(subs, SUB, chans)
    across = jnp.exp(-float(tokens * ROW) * rate)
    before = jnp.exp(-(float(tokens) * place.astype(F32)) * rate)

    @pl.when(is_width_delegate)
    def _():
        pl.semaphore_wait(barrier, n_ten - 1)
        for step in (4, 3, 5, 2, 6, 1, 7):
            signal(width_in, ctx=row * ROW + lax.rem(place + step, ROW))

    wait_bytes(p_in.at[pl.ds(0, ROW - 1)], rs2)

    def from_row(r, carried):
        wait_bytes(c_in.at[r], rsc.at[r])
        return tuple(across[tile_of(j)] * c + c_in[r, j] for j, c in enumerate(carried))

    carried = lax.fori_loop(0, row, from_row, (jnp.zeros((8, LANES), F32),) * tiles)
    for j in range(tiles):
        start = p_in[j] + before[tile_of(j)] * carried[j]
        for s in range(subs):
            states[(s, *tile_of(j))] = states[(s, *tile_of(j))] + decays[(s, *tile_of(j))] * start

    square = jnp.zeros((subs, SUB, LANES), F32)
    for k in range(groups):
        cols = pl.ds(LANES * k, LANES)
        acc = local[:, :, cols]
        for m in range(modes):
            acc = acc + powers[m, :, cols][None] * states[:, pl.ds(m, 1), cols]
        out = q_t[:, :, cols] * acc.astype(jnp.bfloat16).astype(F32)
        square = square + out * out
        go_t[:, :, cols] = out * gain_v[:, cols]

    t_buf[ten] = jnp.sum(square.reshape(tokens, LANES).T, axis=0, keepdims=True)

    @pl.when(jnp.logical_not(is_width_delegate))
    def _():
        pl.semaphore_wait(width_in, 1)

    for step in (10, 6, 14, 9, 11, 2, 8, 5, 7, 13, 15, 1, 3, 4, 12):
        pltpu.make_async_remote_copy(
            t_buf.at[ten], t_buf.at[ten], ss3, rs3,
            device_id={TEN: lax.rem(ten + step, n_ten)}, device_id_type=MESH,
        ).start()

    go_ref[...] = go_t[...].reshape(tokens, chans).T

    wait_bytes(s_buf.at[pl.ds(0, ROW - 1)], ss1)
    wait_bytes(p_out.at[pl.ds(0, ROW - 1)], ss2)
    for later in range(1, n_rows):
        @pl.when(later > row)
        def _():
            wait_bytes(c_in.at[0], ssc.at[later - 1])

    wait_bytes(t_buf.at[pl.ds(0, n_ten - 1)], ss3)
    wait_bytes(t_buf.at[pl.ds(0, n_ten - 1)], rs3)
    scale_ref[...] = lax.rsqrt(jnp.sum(t_buf[...], axis=0) / width + 1e-05)


def body(q_gate, k_gate, values, residues, rates, gain):
    n_ctx, n_ten = lax.axis_size(CTX), lax.axis_size(TEN)
    chans, tokens = q_gate.shape
    modes = rates.shape[1]
    subs, tiles, n_rows = tokens // SUB, modes // 8 * (chans // LANES), n_ctx // ROW
    vmem, dma, regular = pltpu.VMEM, pltpu.SemaphoreType.DMA, pltpu.SemaphoreType.REGULAR
    operands = (q_gate, k_gate, values, residues.T, rates.T, gain.reshape(1, chans))
    operands = [pltpu.with_memory_space_constraint(x, pltpu.HBM) for x in operands]
    gated_out, scale = pl.pallas_call(
        functools.partial(kernel, n_ctx, n_ten, float(chans * n_ten)),
        out_shape=(
            vmem((chans, tokens), F32),
            vmem((1, tokens), F32),
        ),
        in_specs=[pl.BlockSpec(memory_space=pltpu.HBM)] * 6,
        out_specs=(pl.BlockSpec(memory_space=pltpu.VMEM), pl.BlockSpec(memory_space=pltpu.VMEM)),
        scratch_shapes=[
            vmem((chans, tokens), jnp.bfloat16),
            vmem((chans, tokens), jnp.bfloat16),
            vmem((chans, tokens), jnp.bfloat16),
            vmem((modes, chans), F32),
            vmem((modes, chans), F32),
            vmem((1, chans), F32),
            vmem((subs, SUB, chans), F32),
            vmem((subs, 8 + SUB, chans), F32),
            vmem((8 + SUB, chans), F32),
            vmem((modes, SUB, chans), F32),
            vmem((subs, SUB, chans), F32),
            vmem((subs, SUB, chans), F32),
            vmem((subs, modes, chans), F32),
            vmem((subs, modes, chans), F32),
            vmem((tiles, 8, LANES), F32),
            vmem((tiles, 8, LANES), F32),
            vmem((ROW, 8, LANES), F32),
            vmem((ROW, 8, LANES), F32),
            vmem((tiles, 8, LANES), F32),
            vmem((8, LANES), F32),
            vmem((n_rows - 1, tiles, 8, LANES), F32),
            vmem((n_ten, 1, tokens), F32),
            dma((6,)),
            dma(()), dma(()), dma(()), dma(()),
            dma((n_rows - 1,)), dma((n_rows - 1,)),
            dma(()), dma(()),
            regular, regular, regular,
        ],
        compiler_params=pltpu.CompilerParams(
            collective_id=0, has_side_effects=True, vmem_limit_bytes=32 * 1024 * 1024
        ),
        name="hyena",
    )(*operands)
    return (gated_out * scale).astype(jnp.bfloat16)


def solution(mesh):
    return jax.shard_map(
        body,
        mesh=mesh,
        in_specs=(
            P(TEN, CTX),
            P(TEN, CTX),
            P(TEN, CTX),
            P(TEN, None),
            P(TEN, None),
            P(TEN),
        ),
        out_specs=P(TEN, CTX),
        check_vma=False,
    )
```

```python
import functools

import jax
import jax.numpy as jnp
from jax import lax
from jax.experimental import pallas as pl
from jax.experimental.pallas import tpu as pltpu
from jax.sharding import PartitionSpec as P

MESH = pl.DeviceIdType.MESH
CTX, TEN = "context", "tensor"
LANES = 128
SUB = 32
ROW = 8
LATER_DELEGATE = 7
WIDTH_DELEGATE = 5
GREET_ROW = (2, 3, 1, 4, 5, 6, 7)
SEND_ROW = (6, 7, 5, 4, 3, 2, 1)
FAR_WIDTH = (2, 10, 6, 14, 9, 11, 5, 7, 13, 15, 1, 3, 8, 4, 12)
F32 = jnp.float32


def wait_bytes(ref, sem):
    pltpu.make_async_copy(ref, ref, sem).wait()


def kernel(
    n_ctx, n_ten, width,
    q_hbm, k_hbm, v_hbm, res_hbm, rate_hbm, gain_hbm,
    go_ref, scale_ref,
    q_v, k_v, v_v, res_v, rate_v, gain_v, go_t,
    g_pad, taps, powers, local, q_t, states, decays,
    across, before, s_buf, a_buf, r_buf, p_out, p_in, c_out, c_in, t_buf,
    in_sem, ss1, rs1, ss2, rs2, ss_beside, rs_beside, ssc, rsc, ss3, rs3, row_in, later_in, width_in,
):
    me = lax.axis_index(CTX)
    ten = lax.axis_index(TEN)
    modes = rate_hbm.shape[0]
    chans, tokens = q_hbm.shape
    subs = tokens // SUB
    groups = chans // LANES
    halves = modes // 8
    tiles = halves * groups
    n_rows = n_ctx // ROW
    row, place = me >> 3, me & (ROW - 1)
    is_later_delegate = place == LATER_DELEGATE
    is_width_delegate = place == WIDTH_DELEGATE
    beside_delegate = (place == WIDTH_DELEGATE ^ 1) | (place == LATER_DELEGATE ^ 1)
    is_plain = jnp.logical_not(is_later_delegate | is_width_delegate)

    def signal(sem, **where):
        where = {{"ctx": CTX, "ten": TEN}[name]: at for name, at in where.items()}
        pl.semaphore_signal(sem, inc=1, device_id=where, device_id_type=MESH)

    barrier = pltpu.get_barrier_semaphore()
    for step in GREET_ROW:
        other = ((place + step) & (ROW - 1))

        @pl.when((other != LATER_DELEGATE) & (other != WIDTH_DELEGATE))
        def _():
            signal(barrier, ctx=row * ROW + other)

    def greet_earlier(r, carry):
        signal(barrier, ctx=r * ROW + LATER_DELEGATE)
        return carry

    lax.fori_loop(0, row, greet_earlier, 0)

    copies = {}

    def load(name, src, dst, sem):
        copies[name] = pltpu.make_async_copy(src, dst, sem)
        copies[name].start()

    def arrive(name):
        copies[name].wait()

    load("rate", rate_hbm, rate_v, in_sem.at[0])
    load("k", k_hbm, k_v, in_sem.at[1])
    load("v", v_hbm, v_v, in_sem.at[2])
    load("res", res_hbm, res_v, in_sem.at[3])
    load("q", q_hbm, q_v, in_sem.at[4])
    load("gain", gain_hbm, gain_v, in_sem.at[5])

    for step in range(1, n_ten):
        signal(barrier, ctx=row * ROW + WIDTH_DELEGATE, ten=(ten + step) & (n_ten - 1))

    g_pad[...] = jnp.zeros_like(g_pad)
    arrive("rate")
    rate = rate_v[...]
    decay = jnp.exp(-rate)
    decay_sub = jnp.exp(-SUB * rate)
    arrive("k")
    arrive("v")
    gated = (k_v[...].astype(F32) * v_v[...].astype(F32)).astype(jnp.bfloat16).astype(F32)
    g_pad[:, 8:, :] = gated.T.reshape(subs, SUB, chans)

    def advance(i, hs):
        return tuple(decay * h + g_pad[s, pl.ds(8 + i, 1), :] for s, h in enumerate(hs))

    ends = lax.fori_loop(0, SUB, advance, (jnp.zeros((modes, chans), F32),) * subs, unroll=4)
    state = ends[0]
    states[0] = jnp.zeros((modes, chans), F32)
    for s in range(1, subs):
        states[s] = state
        state = decay_sub * state + ends[s]
    decay_all = jnp.exp(-float(tokens) * rate)

    def tile_of(j):
        return slice(8 * (j % halves), 8 * (j % halves) + 8), slice(LANES * (j // halves), LANES * (j // halves) + LANES)

    for j in range(tiles):
        s_buf[j] = state[tile_of(j)]
        a_buf[j] = decay_all[tile_of(j)]

    @pl.when(is_plain)
    def _():
        pl.semaphore_wait(barrier, ROW - 1)

    @pl.when(beside_delegate)
    def _():
        signal(row_in, ctx=row * ROW + (place ^ 1))

    @pl.when(jnp.logical_not(is_plain))
    def _():
        pl.semaphore_wait(row_in, 1)

    for step in SEND_ROW:
        other = ((place + step) & (ROW - 1))
        pltpu.make_async_remote_copy(
            s_buf.at[other], r_buf.at[place], ss1, rs1, device_id={CTX: row * ROW + other}, device_id_type=MESH
        ).start()

    from_beside = pltpu.make_async_remote_copy(
        s_buf, p_in, ss_beside, rs_beside, device_id={CTX: me ^ 1}, device_id_type=MESH
    )

    @pl.when(place == 0)
    def _():
        from_beside.start()

    @pl.when(is_later_delegate)
    def _():
        @pl.when(row < n_rows - 1)
        def _():
            pl.semaphore_wait(barrier, ROW * (n_rows - 1 - row))

        for step in SEND_ROW:
            signal(later_in, ctx=row * ROW + ((place + step) & (ROW - 1)))

    arrive("res")
    weight = res_v[...] * jnp.sqrt(rate)
    ages = (lax.broadcasted_iota(jnp.int32, (SUB, chans), 0) + 1).astype(F32)
    total = jnp.zeros((SUB, chans), F32)
    for m in range(modes):
        power = weight[m : m + 1, :] * jnp.exp(-rate[m : m + 1, :] * ages)
        powers[m] = power
        total = total + power
    taps[7:8, :] = jnp.sum(weight, axis=0, keepdims=True)
    taps[8:, :] = total
    for s in range(subs):
        decays[s] = jnp.exp(-float(SUB * s) * rate)

    def convolve(k, carry):
        cols = pl.ds(pl.multiple_of(k * LANES, LANES), LANES)
        acc = [jnp.zeros((subs, 8, LANES), F32) for _ in range(SUB // 8)]
        for shift in range(8):
            pieces = [g_pad[:, pl.ds(8 + 8 * j - shift, 8), cols] for j in range(SUB // 8)]
            for b in range(SUB // 8):
                tap = taps[pl.ds(7 + 8 * b + shift, 1), cols]
                for j in range(b, SUB // 8):
                    acc[j] = acc[j] + tap * pieces[j - b]
        for j in range(SUB // 8):
            local[:, pl.ds(8 * j, 8), cols] = acc[j]
        return carry

    lax.fori_loop(0, groups, convolve, 0)

    r_buf[place] = s_buf[place]
    wait_bytes(r_buf.at[pl.ds(0, ROW - 1)], rs1)
    ratio = a_buf[place]
    held = jnp.zeros((8, LANES), F32)
    for d in range(ROW):
        p_out[d] = held
        held = ratio * held + r_buf[d]
    c_out[...] = held

    @pl.when(jnp.logical_not(is_later_delegate))
    def _():
        pl.semaphore_wait(later_in, 1)

    for q in range(ROW):
        for later in range(1, n_rows):
            @pl.when(later > row)
            def _():
                pltpu.make_async_remote_copy(
                    c_out, c_in.at[row, place], ssc.at[later - 1], rsc.at[row, place],
                    device_id={CTX: later * ROW + q}, device_id_type=MESH,
                ).start()

        if q >= 2:
            @pl.when(q != place)
            def _():
                pltpu.make_async_remote_copy(
                    p_out.at[q], p_in.at[place], ss2, rs2.at[place], device_id={CTX: row * ROW + q}, device_id_type=MESH
                ).start()

    @pl.when(place >= 2)
    def _():
        p_in[place] = p_out[place]

    @pl.when(place == 0)
    def _():
        p_in[...] = jnp.zeros_like(p_in)

    arrive("q")
    arrive("gain")
    q_t[...] = q_v[...].astype(F32).T.reshape(subs, SUB, chans)
    across[...] = jnp.exp(-float(tokens * ROW) * rate)
    before[...] = jnp.exp(-(float(tokens) * place.astype(F32)) * rate)

    @pl.when(is_width_delegate)
    def _():
        pl.semaphore_wait(barrier, ROW * (n_ten - 1))
        for step in SEND_ROW:
            signal(width_in, ctx=row * ROW + ((place + step) & (ROW - 1)))

    chip = place >> 1

    @pl.when(place == 1)
    def _():
        from_beside.wait_recv()


    def finish(turn, square):
        k = jnp.where(turn == 0, chip, jnp.where(turn <= chip, turn - 1, turn))
        cols = pl.ds(pl.multiple_of(k * LANES, LANES), LANES)
        for i in range(halves):
            j = halves * k + i
            rows = pl.ds(8 * i, 8)

            @pl.when((place >= 2) & (j != place))
            def _():
                wait_bytes(p_in.at[j], rs2.at[j])

            def from_row(r, carried):
                wait_bytes(c_in.at[r, j], rsc.at[r, j])
                return across[rows, cols] * carried + c_in[r, j]

            carried = lax.fori_loop(0, row, from_row, jnp.zeros((8, LANES), F32))
            start = p_in[j] + before[rows, cols] * carried
            for s in range(subs):
                states[s, rows, cols] = states[s, rows, cols] + decays[s, rows, cols] * start
        acc = local[:, :, cols]
        for m in range(modes):
            acc = acc + powers[m, :, cols][None] * states[:, pl.ds(m, 1), cols]
        out = q_t[:, :, cols] * acc.astype(jnp.bfloat16).astype(F32)
        go_t[:, :, cols] = out * gain_v[:, cols]
        return square + out * out

    square = lax.fori_loop(0, groups, finish, jnp.zeros((subs, SUB, LANES), F32))

    t_buf[ten] = jnp.sum(square.reshape(tokens, LANES).T, axis=0, keepdims=True)

    @pl.when(jnp.logical_not(is_width_delegate))
    def _():
        pl.semaphore_wait(width_in, 1)

    for step in FAR_WIDTH:
        pltpu.make_async_remote_copy(
            t_buf.at[ten], t_buf.at[ten], ss3, rs3,
            device_id={TEN: ((ten + step) & (n_ten - 1))}, device_id_type=MESH,
        ).start()

    go_ref[...] = go_t[...].reshape(tokens, chans).T

    wait_bytes(s_buf.at[pl.ds(0, ROW - 1)], ss1)

    @pl.when(place < 2)
    def _():
        wait_bytes(p_out.at[pl.ds(0, ROW - 2)], ss2)

    @pl.when(place >= 2)
    def _():
        wait_bytes(p_out.at[pl.ds(0, ROW - 3)], ss2)

    @pl.when(place == 0)
    def _():
        from_beside.wait_send()

    for later in range(1, n_rows):
        @pl.when(later > row)
        def _():
            wait_bytes(c_in.at[0], ssc.at[later - 1])

    wait_bytes(t_buf.at[pl.ds(0, n_ten - 1)], ss3)
    wait_bytes(t_buf.at[pl.ds(0, n_ten - 1)], rs3)
    scale_ref[...] = lax.rsqrt(jnp.sum(t_buf[...], axis=0) / width + 1e-05)


def body(q_gate, k_gate, values, residues, rates, gain):
    n_ctx, n_ten = lax.axis_size(CTX), lax.axis_size(TEN)
    chans, tokens = q_gate.shape
    modes = rates.shape[1]
    subs, tiles, n_rows = tokens // SUB, modes // 8 * (chans // LANES), n_ctx // ROW
    vmem, dma, regular = pltpu.VMEM, pltpu.SemaphoreType.DMA, pltpu.SemaphoreType.REGULAR
    operands = (q_gate, k_gate, values, residues.T, rates.T, gain.reshape(1, chans))
    operands = [pltpu.with_memory_space_constraint(x, pltpu.HBM) for x in operands]
    gated_out, scale = pl.pallas_call(
        functools.partial(kernel, n_ctx, n_ten, float(chans * n_ten)),
        out_shape=(
            vmem((chans, tokens), F32),
            vmem((1, tokens), F32),
        ),
        in_specs=[pl.BlockSpec(memory_space=pltpu.HBM)] * 6,
        out_specs=(pl.BlockSpec(memory_space=pltpu.VMEM), pl.BlockSpec(memory_space=pltpu.VMEM)),
        scratch_shapes=[
            vmem((chans, tokens), jnp.bfloat16),
            vmem((chans, tokens), jnp.bfloat16),
            vmem((chans, tokens), jnp.bfloat16),
            vmem((modes, chans), F32),
            vmem((modes, chans), F32),
            vmem((1, chans), F32),
            vmem((subs, SUB, chans), F32),
            vmem((subs, 8 + SUB, chans), F32),
            vmem((8 + SUB, chans), F32),
            vmem((modes, SUB, chans), F32),
            vmem((subs, SUB, chans), F32),
            vmem((subs, SUB, chans), F32),
            vmem((subs, modes, chans), F32),
            vmem((subs, modes, chans), F32),
            vmem((modes, chans), F32),
            vmem((modes, chans), F32),
            vmem((tiles, 8, LANES), F32),
            vmem((tiles, 8, LANES), F32),
            vmem((ROW, 8, LANES), F32),
            vmem((ROW, 8, LANES), F32),
            vmem((tiles, 8, LANES), F32),
            vmem((8, LANES), F32),
            vmem((n_rows - 1, tiles, 8, LANES), F32),
            vmem((n_ten, 1, tokens), F32),
            dma((6,)),
            dma(()), dma(()), dma(()), dma((tiles,)), dma(()), dma(()),
            dma((n_rows - 1,)), dma((n_rows - 1, tiles)),
            dma(()), dma(()),
            regular, regular, regular,
        ],
        compiler_params=pltpu.CompilerParams(
            collective_id=0, has_side_effects=True, vmem_limit_bytes=32 * 1024 * 1024
        ),
        name="hyena",
    )(*operands)
    return (gated_out * scale).astype(jnp.bfloat16)


def solution(mesh):
    return jax.shard_map(
        body,
        mesh=mesh,
        in_specs=(
            P(TEN, CTX),
            P(TEN, CTX),
            P(TEN, CTX),
            P(TEN, None),
            P(TEN, None),
            P(TEN),
        ),
        out_specs=P(TEN, CTX),
        check_vma=False,
    )
```

```python
import functools

import jax
import jax.numpy as jnp
from jax import lax
from jax.experimental import pallas as pl
from jax.experimental.pallas import tpu as pltpu
from jax.sharding import PartitionSpec as P

MESH = pl.DeviceIdType.MESH
CTX, TEN = "context", "tensor"
LANES = 128
SUB = 32
ROW = 8
LATER_DELEGATE = 7
WIDTH_DELEGATE = 5
GREET_ROW = (2, 3, 1, 4, 5, 6, 7)
SEND_ROW = (6, 7, 5, 4, 3, 2, 1)
ORDER = (
    (1, 0), (0, 1), (2, 0), (0, 2), (1, 1), (0, 3), (1, 2), (3, 0), (2, 1), (1, 3), (2, 2), (3, 1), (2, 3), (3, 2), (3, 3),
)
FAR_WIDTH = (2, 10, 6, 14, 9, 11, 5, 7, 13, 15, 1, 3, 8, 4, 12)
F32 = jnp.float32


def wait_bytes(ref, sem):
    pltpu.make_async_copy(ref, ref, sem).wait()


def kernel(
    n_ctx, n_ten, width,
    q_hbm, k_hbm, v_hbm, res_hbm, rate_hbm, gain_hbm,
    go_ref, scale_ref,
    q_v, k_v, v_v, res_v, rate_v, gain_v, go_t,
    g_pad, taps, powers, local, q_t, states, decays,
    across, before, s_buf, a_buf, r_buf, p_out, p_in, c_out, c_in, t_buf,
    in_sem, ss1, rs1, ss2, rs2, ss_beside, rs_beside, ssc, rsc, ss3, rs3, row_in, later_in, width_in,
):
    me = lax.axis_index(CTX)
    ten = lax.axis_index(TEN)
    modes = rate_hbm.shape[0]
    chans, tokens = q_hbm.shape
    subs = tokens // SUB
    groups = chans // LANES
    halves = modes // 8
    tiles = halves * groups
    n_rows = n_ctx // ROW
    row, place = me >> 3, me & (ROW - 1)
    is_later_delegate = place == LATER_DELEGATE
    is_width_delegate = place == WIDTH_DELEGATE
    beside_delegate = (place == WIDTH_DELEGATE ^ 1) | (place == LATER_DELEGATE ^ 1)
    is_plain = jnp.logical_not(is_later_delegate | is_width_delegate)

    def signal(sem, **where):
        where = {{"ctx": CTX, "ten": TEN}[name]: at for name, at in where.items()}
        pl.semaphore_signal(sem, inc=1, device_id=where, device_id_type=MESH)

    barrier = pltpu.get_barrier_semaphore()
    for step in GREET_ROW:
        other = ((place + step) & (ROW - 1))

        @pl.when((other != LATER_DELEGATE) & (other != WIDTH_DELEGATE))
        def _():
            signal(barrier, ctx=row * ROW + other)

    def greet_earlier(r, carry):
        signal(barrier, ctx=r * ROW + LATER_DELEGATE)
        return carry

    lax.fori_loop(0, row, greet_earlier, 0)

    copies = {}

    def load(name, src, dst, sem):
        copies[name] = pltpu.make_async_copy(src, dst, sem)
        copies[name].start()

    def arrive(name):
        copies[name].wait()

    load("rate", rate_hbm, rate_v, in_sem.at[0])
    load("k", k_hbm, k_v, in_sem.at[1])
    load("v", v_hbm, v_v, in_sem.at[2])
    load("res", res_hbm, res_v, in_sem.at[3])
    load("q", q_hbm, q_v, in_sem.at[4])
    load("gain", gain_hbm, gain_v, in_sem.at[5])

    for step in range(1, n_ten):
        signal(barrier, ctx=row * ROW + WIDTH_DELEGATE, ten=(ten + step) & (n_ten - 1))

    g_pad[...] = jnp.zeros_like(g_pad)
    arrive("rate")
    rate = rate_v[...]
    decay = jnp.exp(-rate)
    decay_sub = jnp.exp(-SUB * rate)
    arrive("k")
    arrive("v")
    gated = (k_v[...].astype(F32) * v_v[...].astype(F32)).astype(jnp.bfloat16).astype(F32)
    g_pad[:, 8:, :] = gated.T.reshape(subs, SUB, chans)

    def advance(i, hs):
        return tuple(decay * h + g_pad[s, pl.ds(8 + i, 1), :] for s, h in enumerate(hs))

    ends = lax.fori_loop(0, SUB, advance, (jnp.zeros((modes, chans), F32),) * subs, unroll=4)
    state = ends[0]
    states[0] = jnp.zeros((modes, chans), F32)
    for s in range(1, subs):
        states[s] = state
        state = decay_sub * state + ends[s]
    decay_all = jnp.exp(-float(tokens) * rate)

    def tile_of(j):
        return slice(8 * (j % halves), 8 * (j % halves) + 8), slice(LANES * (j // halves), LANES * (j // halves) + LANES)

    for j in range(tiles):
        s_buf[j] = state[tile_of(j)]
        a_buf[j] = decay_all[tile_of(j)]

    @pl.when(is_plain)
    def _():
        pl.semaphore_wait(barrier, ROW - 1)

    @pl.when(beside_delegate)
    def _():
        signal(row_in, ctx=row * ROW + (place ^ 1))

    @pl.when(jnp.logical_not(is_plain))
    def _():
        pl.semaphore_wait(row_in, 1)

    for step in SEND_ROW:
        other = ((place + step) & (ROW - 1))
        pltpu.make_async_remote_copy(
            s_buf.at[other], r_buf.at[place], ss1, rs1, device_id={CTX: row * ROW + other}, device_id_type=MESH
        ).start()

    from_beside = pltpu.make_async_remote_copy(
        s_buf, p_in, ss_beside, rs_beside, device_id={CTX: me ^ 1}, device_id_type=MESH
    )

    @pl.when(place == 0)
    def _():
        from_beside.start()

    @pl.when(is_later_delegate)
    def _():
        @pl.when(row < n_rows - 1)
        def _():
            pl.semaphore_wait(barrier, ROW * (n_rows - 1 - row))

        for step in SEND_ROW:
            signal(later_in, ctx=row * ROW + ((place + step) & (ROW - 1)))

    arrive("res")
    weight = res_v[...] * jnp.sqrt(rate)
    ages = (lax.broadcasted_iota(jnp.int32, (SUB, chans), 0) + 1).astype(F32)
    total = jnp.zeros((SUB, chans), F32)
    for m in range(modes):
        power = weight[m : m + 1, :] * jnp.exp(-rate[m : m + 1, :] * ages)
        powers[m] = power
        total = total + power
    taps[7:8, :] = jnp.sum(weight, axis=0, keepdims=True)
    taps[8:, :] = total
    for s in range(subs):
        decays[s] = jnp.exp(-float(SUB * s) * rate)

    def convolve(k, carry):
        cols = pl.ds(pl.multiple_of(k * LANES, LANES), LANES)
        acc = [jnp.zeros((subs, 8, LANES), F32) for _ in range(SUB // 8)]
        for shift in range(8):
            pieces = [g_pad[:, pl.ds(8 + 8 * j - shift, 8), cols] for j in range(SUB // 8)]
            for b in range(SUB // 8):
                tap = taps[pl.ds(7 + 8 * b + shift, 1), cols]
                for j in range(b, SUB // 8):
                    acc[j] = acc[j] + tap * pieces[j - b]
        for j in range(SUB // 8):
            local[:, pl.ds(8 * j, 8), cols] = acc[j]
        return carry

    lax.fori_loop(0, groups, convolve, 0)

    r_buf[place] = s_buf[place]
    wait_bytes(r_buf.at[pl.ds(0, ROW - 1)], rs1)
    ratio = a_buf[place]
    held = jnp.zeros((8, LANES), F32)
    for d in range(ROW):
        p_out[d] = held
        held = ratio * held + r_buf[d]
    c_out[...] = held

    @pl.when(jnp.logical_not(is_later_delegate))
    def _():
        pl.semaphore_wait(later_in, 1)

    for ahead, chip in ORDER:
        for q in (2 * chip, 2 * chip + 1):
            if ahead:
                @pl.when(row + ahead < n_rows)
                def _():
                    pltpu.make_async_remote_copy(
                        c_out, c_in.at[row, place], ssc.at[ahead - 1], rsc.at[row, place],
                        device_id={CTX: (row + ahead) * ROW + q}, device_id_type=MESH,
                    ).start()
            else:
                @pl.when(q != place)
                def _():
                    pltpu.make_async_remote_copy(
                        p_out.at[q], p_in.at[place], ss2, rs2.at[place], device_id={CTX: row * ROW + q}, device_id_type=MESH
                    ).start()

    @pl.when(place >= 2)
    def _():
        p_in[place] = p_out[place]

    @pl.when(place == 0)
    def _():
        p_in[...] = jnp.zeros_like(p_in)

    arrive("q")
    arrive("gain")
    q_t[...] = q_v[...].astype(F32).T.reshape(subs, SUB, chans)
    across[...] = jnp.exp(-float(tokens * ROW) * rate)
    before[...] = jnp.exp(-(float(tokens) * place.astype(F32)) * rate)

    @pl.when(is_width_delegate)
    def _():
        pl.semaphore_wait(barrier, ROW * (n_ten - 1))
        for step in SEND_ROW:
            signal(width_in, ctx=row * ROW + ((place + step) & (ROW - 1)))

    chip = place >> 1

    @pl.when(place == 1)
    def _():
        from_beside.wait_recv()


    def finish(turn, square):
        k = jnp.where(turn == 0, chip, jnp.where(turn <= chip, turn - 1, turn))
        cols = pl.ds(pl.multiple_of(k * LANES, LANES), LANES)
        for i in range(halves):
            j = halves * k + i
            rows = pl.ds(8 * i, 8)

            @pl.when((place >= 2) & (j != place))
            def _():
                wait_bytes(p_in.at[j], rs2.at[j])

            def from_row(r, carried):
                wait_bytes(c_in.at[r, j], rsc.at[r, j])
                return across[rows, cols] * carried + c_in[r, j]

            carried = lax.fori_loop(0, row, from_row, jnp.zeros((8, LANES), F32))
            start = p_in[j] + before[rows, cols] * carried
            for s in range(subs):
                states[s, rows, cols] = states[s, rows, cols] + decays[s, rows, cols] * start
        acc = local[:, :, cols]
        for m in range(modes):
            acc = acc + powers[m, :, cols][None] * states[:, pl.ds(m, 1), cols]
        out = q_t[:, :, cols] * acc.astype(jnp.bfloat16).astype(F32)
        go_t[:, :, cols] = out * gain_v[:, cols]
        return square + out * out

    square = lax.fori_loop(0, groups, finish, jnp.zeros((subs, SUB, LANES), F32))

    t_buf[ten] = jnp.sum(square.reshape(tokens, LANES).T, axis=0, keepdims=True)

    @pl.when(jnp.logical_not(is_width_delegate))
    def _():
        pl.semaphore_wait(width_in, 1)

    for step in FAR_WIDTH:
        pltpu.make_async_remote_copy(
            t_buf.at[ten], t_buf.at[ten], ss3, rs3,
            device_id={TEN: ((ten + step) & (n_ten - 1))}, device_id_type=MESH,
        ).start()

    go_ref[...] = go_t[...].reshape(tokens, chans).T

    wait_bytes(s_buf.at[pl.ds(0, ROW - 1)], ss1)

    @pl.when(place < 2)
    def _():
        wait_bytes(p_out.at[pl.ds(0, ROW - 2)], ss2)

    @pl.when(place >= 2)
    def _():
        wait_bytes(p_out.at[pl.ds(0, ROW - 3)], ss2)

    @pl.when(place == 0)
    def _():
        from_beside.wait_send()

    for later in range(1, n_rows):
        @pl.when(row + later < n_rows)
        def _():
            wait_bytes(c_in.at[0], ssc.at[later - 1])

    wait_bytes(t_buf.at[pl.ds(0, n_ten - 1)], ss3)
    wait_bytes(t_buf.at[pl.ds(0, n_ten - 1)], rs3)
    scale_ref[...] = lax.rsqrt(jnp.sum(t_buf[...], axis=0) / width + 1e-05)


def body(q_gate, k_gate, values, residues, rates, gain):
    n_ctx, n_ten = lax.axis_size(CTX), lax.axis_size(TEN)
    chans, tokens = q_gate.shape
    modes = rates.shape[1]
    subs, tiles, n_rows = tokens // SUB, modes // 8 * (chans // LANES), n_ctx // ROW
    vmem, dma, regular = pltpu.VMEM, pltpu.SemaphoreType.DMA, pltpu.SemaphoreType.REGULAR
    operands = (q_gate, k_gate, values, residues.T, rates.T, gain.reshape(1, chans))
    operands = [pltpu.with_memory_space_constraint(x, pltpu.HBM) for x in operands]
    gated_out, scale = pl.pallas_call(
        functools.partial(kernel, n_ctx, n_ten, float(chans * n_ten)),
        out_shape=(
            vmem((chans, tokens), F32),
            vmem((1, tokens), F32),
        ),
        in_specs=[pl.BlockSpec(memory_space=pltpu.HBM)] * 6,
        out_specs=(pl.BlockSpec(memory_space=pltpu.VMEM), pl.BlockSpec(memory_space=pltpu.VMEM)),
        scratch_shapes=[
            vmem((chans, tokens), jnp.bfloat16),
            vmem((chans, tokens), jnp.bfloat16),
            vmem((chans, tokens), jnp.bfloat16),
            vmem((modes, chans), F32),
            vmem((modes, chans), F32),
            vmem((1, chans), F32),
            vmem((subs, SUB, chans), F32),
            vmem((subs, 8 + SUB, chans), F32),
            vmem((8 + SUB, chans), F32),
            vmem((modes, SUB, chans), F32),
            vmem((subs, SUB, chans), F32),
            vmem((subs, SUB, chans), F32),
            vmem((subs, modes, chans), F32),
            vmem((subs, modes, chans), F32),
            vmem((modes, chans), F32),
            vmem((modes, chans), F32),
            vmem((tiles, 8, LANES), F32),
            vmem((tiles, 8, LANES), F32),
            vmem((ROW, 8, LANES), F32),
            vmem((ROW, 8, LANES), F32),
            vmem((tiles, 8, LANES), F32),
            vmem((8, LANES), F32),
            vmem((n_rows - 1, tiles, 8, LANES), F32),
            vmem((n_ten, 1, tokens), F32),
            dma((6,)),
            dma(()), dma(()), dma(()), dma((tiles,)), dma(()), dma(()),
            dma((n_rows - 1,)), dma((n_rows - 1, tiles)),
            dma(()), dma(()),
            regular, regular, regular,
        ],
        compiler_params=pltpu.CompilerParams(
            collective_id=0, has_side_effects=True, vmem_limit_bytes=32 * 1024 * 1024
        ),
        name="hyena",
    )(*operands)
    return (gated_out * scale).astype(jnp.bfloat16)


def solution(mesh):
    return jax.shard_map(
        body,
        mesh=mesh,
        in_specs=(
            P(TEN, CTX),
            P(TEN, CTX),
            P(TEN, CTX),
            P(TEN, None),
            P(TEN, None),
            P(TEN),
        ),
        out_specs=P(TEN, CTX),
        check_vma=False,
    )
```

```python
import functools

import jax
import jax.numpy as jnp
from jax import lax
from jax.experimental import pallas as pl
from jax.experimental.pallas import tpu as pltpu
from jax.sharding import PartitionSpec as P

MESH = pl.DeviceIdType.MESH
CTX, TEN = "context", "tensor"
LANES = 128
SUB = 32
ROW = 8
LATER_DELEGATE = 7
WIDTH_DELEGATE = 5
GREET_ROW = (2, 3, 1, 4, 5, 6, 7)
SEND_ROW = (6, 7, 5, 4, 3, 2, 1)
ORDER = (
    (1, 0), (0, 1), (2, 0), (0, 2), (1, 1), (0, 3), (1, 2), (3, 0), (2, 1), (1, 3), (2, 2), (3, 1), (2, 3), (3, 2), (3, 3),
)
FAR_WIDTH = (2, 10, 6, 14, 9, 11, 5, 7, 13, 15, 1, 3, 8, 4, 12)
F32 = jnp.float32


def wait_bytes(ref, sem):
    pltpu.make_async_copy(ref, ref, sem).wait()


def kernel(
    n_ctx, n_ten, width,
    q_hbm, k_hbm, v_hbm, res_hbm, rate_hbm, gain_hbm,
    go_ref, scale_ref,
    q_v, kv_v, poles_v, gain_v, go_t,
    g_pad, taps, powers, local, q_t, states, decays,
    across, before, s_buf, a_buf, r_buf, p_out, c_out, arrived, t_buf,
    poles_sem, kv_sem, q_sem, gain_sem, rs1, group_sem, sent_sem, ss3, rs3, row_in, later_in, width_in,
):
    me = lax.axis_index(CTX)
    ten = lax.axis_index(TEN)
    modes = rate_hbm.shape[0]
    chans, tokens = q_hbm.shape
    subs = tokens // SUB
    groups = chans // LANES
    halves = modes // 8
    tiles = halves * groups
    n_rows = n_ctx // ROW
    prefixes = (n_rows - 1) * tiles
    row, place = me >> 3, me & (ROW - 1)
    is_later_delegate = place == LATER_DELEGATE
    is_width_delegate = place == WIDTH_DELEGATE
    beside_delegate = (place == WIDTH_DELEGATE ^ 1) | (place == LATER_DELEGATE ^ 1)
    is_plain = jnp.logical_not(is_later_delegate | is_width_delegate)

    def signal(sem, **where):
        where = {{"ctx": CTX, "ten": TEN}[name]: at for name, at in where.items()}
        pl.semaphore_signal(sem, inc=1, device_id=where, device_id_type=MESH)

    barrier = pltpu.get_barrier_semaphore()
    for step in GREET_ROW:
        other = ((place + step) & (ROW - 1))

        @pl.when((other != LATER_DELEGATE) & (other != WIDTH_DELEGATE))
        def _():
            signal(barrier, ctx=row * ROW + other)

    def greet_earlier(r, carry):
        signal(barrier, ctx=r * ROW + LATER_DELEGATE)
        return carry

    lax.fori_loop(0, row, greet_earlier, 0)

    for src, dst, sem in (
        (rate_hbm, poles_v.at[0], poles_sem), (res_hbm, poles_v.at[1], poles_sem),
        (k_hbm, kv_v.at[0], kv_sem), (v_hbm, kv_v.at[1], kv_sem),
        (q_hbm, q_v, q_sem), (gain_hbm, gain_v, gain_sem),
    ):
        pltpu.make_async_copy(src, dst, sem).start()

    for step in range(1, n_ten):
        signal(barrier, ctx=row * ROW + WIDTH_DELEGATE, ten=(ten + step) & (n_ten - 1))

    g_pad[...] = jnp.zeros_like(g_pad)
    wait_bytes(poles_v, poles_sem)
    rate = poles_v[0]
    decay = jnp.exp(-rate)
    decay_sub = jnp.exp(-SUB * rate)
    wait_bytes(kv_v, kv_sem)
    gated = (kv_v[0].astype(F32) * kv_v[1].astype(F32)).astype(jnp.bfloat16).astype(F32)
    g_pad[:, 8:, :] = gated.T.reshape(subs, SUB, chans)

    def advance(i, hs):
        return tuple(decay * h + g_pad[s, pl.ds(8 + i, 1), :] for s, h in enumerate(hs))

    ends = lax.fori_loop(0, SUB, advance, (jnp.zeros((modes, chans), F32),) * subs, unroll=4)
    state = ends[0]
    states[0] = jnp.zeros((modes, chans), F32)
    for s in range(1, subs):
        states[s] = state
        state = decay_sub * state + ends[s]
    decay_all = jnp.exp(-float(tokens) * rate)

    def tile_of(j):
        return slice(8 * (j % halves), 8 * (j % halves) + 8), slice(LANES * (j // halves), LANES * (j // halves) + LANES)

    for j in range(tiles):
        s_buf[j] = state[tile_of(j)]
        a_buf[j] = decay_all[tile_of(j)]

    @pl.when(is_plain)
    def _():
        pl.semaphore_wait(barrier, ROW - 1)

    @pl.when(beside_delegate)
    def _():
        signal(row_in, ctx=row * ROW + (place ^ 1))

    @pl.when(jnp.logical_not(is_plain))
    def _():
        pl.semaphore_wait(row_in, 1)

    for step in SEND_ROW:
        other = ((place + step) & (ROW - 1))
        pltpu.make_async_remote_copy(
            s_buf.at[other], r_buf.at[place], sent_sem, rs1, device_id={CTX: row * ROW + other}, device_id_type=MESH
        ).start()

    from_beside = pltpu.make_async_remote_copy(
        s_buf, arrived.at[pl.ds(prefixes, tiles)], sent_sem, rs1, device_id={CTX: me ^ 1}, device_id_type=MESH
    )

    @pl.when(place == 0)
    def _():
        from_beside.start()

    @pl.when(is_later_delegate)
    def _():
        @pl.when(row < n_rows - 1)
        def _():
            pl.semaphore_wait(barrier, ROW * (n_rows - 1 - row))

        for step in SEND_ROW:
            signal(later_in, ctx=row * ROW + ((place + step) & (ROW - 1)))

    weight = poles_v[1] * jnp.sqrt(rate)
    ages = (lax.broadcasted_iota(jnp.int32, (SUB, chans), 0) + 1).astype(F32)
    total = jnp.zeros((SUB, chans), F32)
    for m in range(modes):
        power = weight[m : m + 1, :] * jnp.exp(-rate[m : m + 1, :] * ages)
        powers[m] = power
        total = total + power
    taps[7:8, :] = jnp.sum(weight, axis=0, keepdims=True)
    taps[8:, :] = total
    for s in range(subs):
        decays[s] = jnp.exp(-float(SUB * s) * rate)

    def convolve(k, carry):
        cols = pl.ds(pl.multiple_of(k * LANES, LANES), LANES)
        acc = [jnp.zeros((subs, 8, LANES), F32) for _ in range(SUB // 8)]
        for shift in range(8):
            pieces = [g_pad[:, pl.ds(8 + 8 * j - shift, 8), cols] for j in range(SUB // 8)]
            for b in range(SUB // 8):
                tap = taps[pl.ds(7 + 8 * b + shift, 1), cols]
                for j in range(b, SUB // 8):
                    acc[j] = acc[j] + tap * pieces[j - b]
        for j in range(SUB // 8):
            local[:, pl.ds(8 * j, 8), cols] = acc[j]
        return carry

    lax.fori_loop(0, groups, convolve, 0)

    r_buf[place] = s_buf[place]
    @pl.when(place == 1)
    def _():
        wait_bytes(arrived.at[pl.ds(0, ROW - 1 + tiles)], rs1)

    @pl.when(place != 1)
    def _():
        wait_bytes(arrived.at[pl.ds(0, ROW - 1)], rs1)

    ratio = a_buf[place]
    held = jnp.zeros((8, LANES), F32)
    for d in range(ROW):
        p_out[d] = held
        held = ratio * held + r_buf[d]
    c_out[...] = held

    @pl.when(jnp.logical_not(is_later_delegate))
    def _():
        pl.semaphore_wait(later_in, 1)

    for ahead, chip in ORDER:
        for q in (2 * chip, 2 * chip + 1):
            if ahead:
                @pl.when(row + ahead < n_rows)
                def _():
                    pltpu.make_async_remote_copy(
                        c_out, arrived.at[tiles * row + place], sent_sem, group_sem.at[place >> 1],
                        device_id={CTX: (row + ahead) * ROW + q}, device_id_type=MESH,
                    ).start()
            else:
                @pl.when(q != place)
                def _():
                    pltpu.make_async_remote_copy(
                        p_out.at[q], arrived.at[prefixes + place], sent_sem, group_sem.at[place >> 1], device_id={CTX: row * ROW + q}, device_id_type=MESH
                    ).start()

    @pl.when(place >= 2)
    def _():
        arrived[prefixes + place] = p_out[place]

    @pl.when(place == 0)
    def _():
        arrived[prefixes : prefixes + tiles] = jnp.zeros((tiles, 8, LANES), F32)

    wait_bytes(q_v, q_sem)
    wait_bytes(gain_v, gain_sem)
    q_t[...] = q_v[...].astype(F32).T.reshape(subs, SUB, chans)
    across[...] = jnp.exp(-float(tokens * ROW) * rate)
    before[...] = jnp.exp(-(float(tokens) * place.astype(F32)) * rate)

    @pl.when(is_width_delegate)
    def _():
        pl.semaphore_wait(barrier, ROW * (n_ten - 1))
        for step in SEND_ROW:
            signal(width_in, ctx=row * ROW + ((place + step) & (ROW - 1)))

    chip = place >> 1


    def finish(turn, square):
        k = jnp.where(turn == 0, chip, jnp.where(turn <= chip, turn - 1, turn))
        cols = pl.ds(pl.multiple_of(k * LANES, LANES), LANES)
        count = halves * row + jnp.where(place < 2, 0, jnp.where(k == chip, halves - 1, halves))
        for tiles_in in range(1, halves * n_rows + 1):
            @pl.when(count == tiles_in)
            def _():
                wait_bytes(arrived.at[pl.ds(0, tiles_in)], group_sem.at[k])

        for i in range(halves):
            j = halves * k + i
            rows = pl.ds(8 * i, 8)

            def from_row(r, carried):
                return across[rows, cols] * carried + arrived[tiles * r + j]

            carried = lax.fori_loop(0, row, from_row, jnp.zeros((8, LANES), F32))
            start = arrived[prefixes + j] + before[rows, cols] * carried
            for s in range(subs):
                states[s, rows, cols] = states[s, rows, cols] + decays[s, rows, cols] * start
        acc = local[:, :, cols]
        for m in range(modes):
            acc = acc + powers[m, :, cols][None] * states[:, pl.ds(m, 1), cols]
        out = q_t[:, :, cols] * acc.astype(jnp.bfloat16).astype(F32)
        go_t[:, :, cols] = out * gain_v[:, cols]
        return square + out * out

    square = lax.fori_loop(0, groups, finish, jnp.zeros((subs, SUB, LANES), F32))

    t_buf[ten] = jnp.sum(square.reshape(tokens, LANES).T, axis=0, keepdims=True)

    @pl.when(jnp.logical_not(is_width_delegate))
    def _():
        pl.semaphore_wait(width_in, 1)

    for step in FAR_WIDTH:
        pltpu.make_async_remote_copy(
            t_buf.at[ten], t_buf.at[ten], ss3, rs3,
            device_id={TEN: ((ten + step) & (n_ten - 1))}, device_id_type=MESH,
        ).start()

    go_ref[...] = go_t[...].reshape(tokens, chans).T

    for r in range(n_rows):
        for first, last, prefix_tiles in ((0, 0, tiles + ROW - 2), (1, 1, ROW - 2), (2, ROW - 1, ROW - 3)):
            @pl.when((row == r) & (place >= first) & (place <= last))
            def _():
                wait_bytes(arrived.at[pl.ds(0, ROW - 1 + prefix_tiles + ROW * (n_rows - 1 - r))], sent_sem)

    wait_bytes(t_buf.at[pl.ds(0, n_ten - 1)], ss3)
    wait_bytes(t_buf.at[pl.ds(0, n_ten - 1)], rs3)
    scale_ref[...] = lax.rsqrt(jnp.sum(t_buf[...], axis=0) / width + 1e-05)


def body(q_gate, k_gate, values, residues, rates, gain):
    n_ctx, n_ten = lax.axis_size(CTX), lax.axis_size(TEN)
    chans, tokens = q_gate.shape
    modes = rates.shape[1]
    subs, tiles, n_rows = tokens // SUB, modes // 8 * (chans // LANES), n_ctx // ROW
    vmem, dma, regular = pltpu.VMEM, pltpu.SemaphoreType.DMA, pltpu.SemaphoreType.REGULAR
    operands = (q_gate, k_gate, values, residues.T, rates.T, gain.reshape(1, chans))
    operands = [pltpu.with_memory_space_constraint(x, pltpu.HBM) for x in operands]
    gated_out, scale = pl.pallas_call(
        functools.partial(kernel, n_ctx, n_ten, float(chans * n_ten)),
        out_shape=(
            vmem((chans, tokens), F32),
            vmem((1, tokens), F32),
        ),
        in_specs=[pl.BlockSpec(memory_space=pltpu.HBM)] * 6,
        out_specs=(pl.BlockSpec(memory_space=pltpu.VMEM), pl.BlockSpec(memory_space=pltpu.VMEM)),
        scratch_shapes=[
            vmem((chans, tokens), jnp.bfloat16),
            vmem((2, chans, tokens), jnp.bfloat16),
            vmem((2, modes, chans), F32),
            vmem((1, chans), F32),
            vmem((subs, SUB, chans), F32),
            vmem((subs, 8 + SUB, chans), F32),
            vmem((8 + SUB, chans), F32),
            vmem((modes, SUB, chans), F32),
            vmem((subs, SUB, chans), F32),
            vmem((subs, SUB, chans), F32),
            vmem((subs, modes, chans), F32),
            vmem((subs, modes, chans), F32),
            vmem((modes, chans), F32),
            vmem((modes, chans), F32),
            vmem((tiles, 8, LANES), F32),
            vmem((tiles, 8, LANES), F32),
            vmem((ROW, 8, LANES), F32),
            vmem((ROW, 8, LANES), F32),
            vmem((8, LANES), F32),
            vmem((2 * tiles + 2 * ROW + ROW * n_rows, 8, LANES), F32),
            vmem((n_ten, 1, tokens), F32),
            dma(()), dma(()), dma(()), dma(()),
            dma(()), dma((chans // LANES,)), dma(()), dma(()), dma(()),
            regular, regular, regular,
        ],
        compiler_params=pltpu.CompilerParams(
            collective_id=0, has_side_effects=True, vmem_limit_bytes=32 * 1024 * 1024
        ),
        name="hyena",
    )(*operands)
    return (gated_out * scale).astype(jnp.bfloat16)


def solution(mesh):
    return jax.shard_map(
        body,
        mesh=mesh,
        in_specs=(
            P(TEN, CTX),
            P(TEN, CTX),
            P(TEN, CTX),
            P(TEN, None),
            P(TEN, None),
            P(TEN),
        ),
        out_specs=P(TEN, CTX),
        check_vma=False,
    )
```

```python
import functools

import jax
import jax.numpy as jnp
from jax import lax
from jax.experimental import pallas as pl
from jax.experimental.pallas import tpu as pltpu
from jax.sharding import PartitionSpec as P

MESH = pl.DeviceIdType.MESH
CTX, TEN = "context", "tensor"
LANES = 128
SUB = 32
ROW = 8
LATER_DELEGATE = 7
WIDTH_DELEGATE = 5
GREET_ROW = (2, 3, 1, 4, 5, 6, 7)
SEND_ROW = (6, 7, 5, 4, 3, 2, 1)
ORDER = ((1, 0), (1, 1), (2, 0), (2, 1), (3, 0), (3, 1))
FAR_WIDTH = (2, 10, 6, 14, 9, 11, 5, 7, 13, 15, 1, 3, 8, 4, 12)
F32 = jnp.float32


def wait_bytes(ref, sem):
    pltpu.make_async_copy(ref, ref, sem).wait()


def kernel(
    n_ctx, n_ten, width,
    q_hbm, k_hbm, v_hbm, res_hbm, rate_hbm, gain_hbm,
    go_ref, scale_ref,
    q_v, kv_v, poles_v, gain_v, go_t,
    g_pad, taps, powers, local, q_t, states, decays,
    across, before, s_buf, a_buf, r_buf, p_out, c_out, arrived, t_buf,
    poles_sem, kv_sem, q_sem, gain_sem, rs1, group_sem, sent_sem, ss3, rs3, row_in, later_in, width_in,
):
    me = lax.axis_index(CTX)
    ten = lax.axis_index(TEN)
    modes = rate_hbm.shape[0]
    chans, tokens = q_hbm.shape
    subs = tokens // SUB
    groups = chans // LANES
    n_rows = n_ctx // ROW
    prefixes = (n_rows - 1) * groups
    half = groups
    row, place = me >> 3, me & (ROW - 1)
    mine = place & (half - 1)
    is_later_delegate = place == LATER_DELEGATE
    is_width_delegate = place == WIDTH_DELEGATE
    beside_delegate = (place == WIDTH_DELEGATE ^ 1) | (place == LATER_DELEGATE ^ 1)
    is_plain = jnp.logical_not(is_later_delegate | is_width_delegate)

    def signal(sem, **where):
        where = {{"ctx": CTX, "ten": TEN}[name]: at for name, at in where.items()}
        pl.semaphore_signal(sem, inc=1, device_id=where, device_id_type=MESH)

    barrier = pltpu.get_barrier_semaphore()
    for step in GREET_ROW:
        other = ((place + step) & (ROW - 1))

        @pl.when((other != LATER_DELEGATE) & (other != WIDTH_DELEGATE))
        def _():
            signal(barrier, ctx=row * ROW + other)

    def greet_earlier(r, carry):
        signal(barrier, ctx=r * ROW + LATER_DELEGATE)
        return carry

    lax.fori_loop(0, row, greet_earlier, 0)

    for src, dst, sem in (
        (rate_hbm, poles_v.at[0], poles_sem), (res_hbm, poles_v.at[1], poles_sem),
        (k_hbm, kv_v.at[0], kv_sem), (v_hbm, kv_v.at[1], kv_sem),
        (q_hbm, q_v, q_sem), (gain_hbm, gain_v, gain_sem),
    ):
        pltpu.make_async_copy(src, dst, sem).start()

    for step in range(1, n_ten):
        signal(barrier, ctx=row * ROW + WIDTH_DELEGATE, ten=(ten + step) & (n_ten - 1))

    g_pad[...] = jnp.zeros_like(g_pad)
    wait_bytes(poles_v, poles_sem)
    rate = poles_v[0]
    decay = jnp.exp(-rate)
    decay_sub = jnp.exp(-SUB * rate)
    wait_bytes(kv_v, kv_sem)
    gated = (kv_v[0].astype(F32) * kv_v[1].astype(F32)).astype(jnp.bfloat16).astype(F32)
    g_pad[:, 8:, :] = gated.T.reshape(subs, SUB, chans)

    def advance(i, hs):
        return tuple(decay * h + g_pad[s, pl.ds(8 + i, 1), :] for s, h in enumerate(hs))

    ends = lax.fori_loop(0, SUB, advance, (jnp.zeros((modes, chans), F32),) * subs, unroll=4)
    state = ends[0]
    states[0] = jnp.zeros((modes, chans), F32)
    for s in range(1, subs):
        states[s] = state
        state = decay_sub * state + ends[s]
    decay_all = jnp.exp(-float(tokens) * rate)

    for g in range(groups):
        s_buf[g] = state[:, LANES * g : LANES * (g + 1)]
        a_buf[g] = decay_all[:, LANES * g : LANES * (g + 1)]

    @pl.when(is_plain)
    def _():
        pl.semaphore_wait(barrier, ROW - 1)

    @pl.when(beside_delegate)
    def _():
        signal(row_in, ctx=row * ROW + (place ^ 1))

    @pl.when(jnp.logical_not(is_plain))
    def _():
        pl.semaphore_wait(row_in, 1)

    for step in SEND_ROW:
        other = ((place + step) & (ROW - 1))
        pltpu.make_async_remote_copy(
            s_buf.at[other & (half - 1)], r_buf.at[place], sent_sem, rs1.at[place >> 2], device_id={CTX: row * ROW + other}, device_id_type=MESH
        ).start()

    from_beside = pltpu.make_async_remote_copy(
        s_buf, arrived.at[pl.ds(prefixes, groups)], sent_sem, rs1.at[0], device_id={CTX: me ^ 1}, device_id_type=MESH
    )

    @pl.when(place == 0)
    def _():
        from_beside.start()

    @pl.when(is_later_delegate)
    def _():
        @pl.when(row < n_rows - 1)
        def _():
            pl.semaphore_wait(barrier, ROW * (n_rows - 1 - row))

        for step in SEND_ROW:
            signal(later_in, ctx=row * ROW + ((place + step) & (ROW - 1)))

    weight = poles_v[1] * jnp.sqrt(rate)
    ages = (lax.broadcasted_iota(jnp.int32, (SUB, chans), 0) + 1).astype(F32)
    total = jnp.zeros((SUB, chans), F32)
    for m in range(modes):
        power = weight[m : m + 1, :] * jnp.exp(-rate[m : m + 1, :] * ages)
        powers[m] = power
        total = total + power
    taps[7:8, :] = jnp.sum(weight, axis=0, keepdims=True)
    taps[8:, :] = total
    for s in range(subs):
        decays[s] = jnp.exp(-float(SUB * s) * rate)

    def convolve(k, carry):
        cols = pl.ds(pl.multiple_of(k * LANES, LANES), LANES)
        acc = [jnp.zeros((subs, 8, LANES), F32) for _ in range(SUB // 8)]
        for shift in range(8):
            pieces = [g_pad[:, pl.ds(8 + 8 * j - shift, 8), cols] for j in range(SUB // 8)]
            for b in range(SUB // 8):
                tap = taps[pl.ds(7 + 8 * b + shift, 1), cols]
                for j in range(b, SUB // 8):
                    acc[j] = acc[j] + tap * pieces[j - b]
        for j in range(SUB // 8):
            local[:, pl.ds(8 * j, 8), cols] = acc[j]
        return carry

    lax.fori_loop(0, groups, convolve, 0)

    r_buf[place] = s_buf[mine]

    ratio = a_buf[mine]

    def scan(held, first):
        for d in range(first, first + half):
            p_out[d] = held
            held = ratio * held + r_buf[d]
        return held

    def give_prefixes():
        for step in range(1, half):
            q = (place & half) + ((place + step) & (half - 1))

            @pl.when(q >= 2)
            def _():
                pltpu.make_async_remote_copy(
                    p_out.at[q], arrived.at[prefixes + mine], sent_sem, group_sem.at[mine],
                    device_id={CTX: row * ROW + q}, device_id_type=MESH,
                ).start()

    for units, here in ((half - 1 + groups, place == 1), (half - 1, (place < half) & (place != 1)), (half, place >= half)):
        @pl.when(here)
        def _():
            wait_bytes(arrived.at[pl.ds(0, units)], rs1.at[0])

    held = scan(jnp.zeros((modes, LANES), F32), 0)

    @pl.when(place < half)
    def _():
        give_prefixes()
        wait_bytes(arrived.at[pl.ds(0, half)], rs1.at[1])

    @pl.when(place >= half)
    def _():
        wait_bytes(arrived.at[pl.ds(0, half - 1)], rs1.at[1])

    c_out[...] = scan(held, half)

    @pl.when(place >= half)
    def _():
        give_prefixes()

    @pl.when(jnp.logical_not(is_later_delegate))
    def _():
        pl.semaphore_wait(later_in, 1)

    for ahead, chip in ORDER:
        for core in range(2):
            @pl.when(row + ahead < n_rows)
            def _():
                pltpu.make_async_remote_copy(
                    c_out, arrived.at[groups * row + mine], sent_sem, group_sem.at[mine],
                    device_id={CTX: (row + ahead) * ROW + (place & half) + 2 * chip + core}, device_id_type=MESH,
                ).start()

    @pl.when(place >= 2)
    def _():
        arrived[prefixes + mine] = p_out[place]

    @pl.when(place == 0)
    def _():
        arrived[prefixes : prefixes + groups] = jnp.zeros((groups, modes, LANES), F32)

    wait_bytes(q_v, q_sem)
    wait_bytes(gain_v, gain_sem)
    q_t[...] = q_v[...].astype(F32).T.reshape(subs, SUB, chans)
    across[...] = jnp.exp(-float(tokens * ROW) * rate)
    before[...] = jnp.exp(-(float(tokens) * place.astype(F32)) * rate)

    @pl.when(is_width_delegate)
    def _():
        pl.semaphore_wait(barrier, ROW * (n_ten - 1))
        for step in SEND_ROW:
            signal(width_in, ctx=row * ROW + ((place + step) & (ROW - 1)))

    def finish(turn, square):
        g = (place & 2) ^ turn
        cols = pl.ds(pl.multiple_of(g * LANES, LANES), LANES)
        count = row + jnp.where((place >= 2) & (g != mine), 1, 0)
        for units in range(1, n_rows + 1):
            @pl.when(count == units)
            def _():
                wait_bytes(arrived.at[pl.ds(0, units)], group_sem.at[g])

        def from_row(r, carried):
            return across[:, cols] * carried + arrived[groups * r + g]

        carried = lax.fori_loop(0, row, from_row, jnp.zeros((modes, LANES), F32))
        start = arrived[prefixes + g] + before[:, cols] * carried
        for s in range(subs):
            states[s, :, cols] = states[s, :, cols] + decays[s, :, cols] * start
        acc = local[:, :, cols]
        for m in range(modes):
            acc = acc + powers[m, :, cols][None] * states[:, pl.ds(m, 1), cols]
        out = q_t[:, :, cols] * acc.astype(jnp.bfloat16).astype(F32)
        go_t[:, :, cols] = out * gain_v[:, cols]
        return square + out * out

    square = lax.fori_loop(0, groups, finish, jnp.zeros((subs, SUB, LANES), F32))

    t_buf[ten] = jnp.sum(square.reshape(tokens, LANES).T, axis=0, keepdims=True)

    @pl.when(jnp.logical_not(is_width_delegate))
    def _():
        pl.semaphore_wait(width_in, 1)

    for step in FAR_WIDTH:
        pltpu.make_async_remote_copy(
            t_buf.at[ten], t_buf.at[ten], ss3, rs3,
            device_id={TEN: ((ten + step) & (n_ten - 1))}, device_id_type=MESH,
        ).start()

    go_ref[...] = go_t[...].reshape(tokens, chans).T

    for r in range(n_rows):
        for first, last, prefix_units in ((0, 0, groups + 2), (1, 1, 2), (2, 3, 1), (4, 7, 3)):
            @pl.when((row == r) & (place >= first) & (place <= last))
            def _():
                wait_bytes(arrived.at[pl.ds(0, ROW - 1 + prefix_units + half * (n_rows - 1 - r))], sent_sem)

    wait_bytes(t_buf.at[pl.ds(0, n_ten - 1)], ss3)
    wait_bytes(t_buf.at[pl.ds(0, n_ten - 1)], rs3)
    scale_ref[...] = lax.rsqrt(jnp.sum(t_buf[...], axis=0) / width + 1e-05)


def body(q_gate, k_gate, values, residues, rates, gain):
    n_ctx, n_ten = lax.axis_size(CTX), lax.axis_size(TEN)
    chans, tokens = q_gate.shape
    modes = rates.shape[1]
    subs, groups, n_rows = tokens // SUB, chans // LANES, n_ctx // ROW
    vmem, dma, regular = pltpu.VMEM, pltpu.SemaphoreType.DMA, pltpu.SemaphoreType.REGULAR
    operands = (q_gate, k_gate, values, residues.T, rates.T, gain.reshape(1, chans))
    operands = [pltpu.with_memory_space_constraint(x, pltpu.HBM) for x in operands]
    gated_out, scale = pl.pallas_call(
        functools.partial(kernel, n_ctx, n_ten, float(chans * n_ten)),
        out_shape=(
            vmem((chans, tokens), F32),
            vmem((1, tokens), F32),
        ),
        in_specs=[pl.BlockSpec(memory_space=pltpu.HBM)] * 6,
        out_specs=(pl.BlockSpec(memory_space=pltpu.VMEM), pl.BlockSpec(memory_space=pltpu.VMEM)),
        scratch_shapes=[
            vmem((chans, tokens), jnp.bfloat16),
            vmem((2, chans, tokens), jnp.bfloat16),
            vmem((2, modes, chans), F32),
            vmem((1, chans), F32),
            vmem((subs, SUB, chans), F32),
            vmem((subs, 8 + SUB, chans), F32),
            vmem((8 + SUB, chans), F32),
            vmem((modes, SUB, chans), F32),
            vmem((subs, SUB, chans), F32),
            vmem((subs, SUB, chans), F32),
            vmem((subs, modes, chans), F32),
            vmem((subs, modes, chans), F32),
            vmem((modes, chans), F32),
            vmem((modes, chans), F32),
            vmem((groups, modes, LANES), F32),
            vmem((groups, modes, LANES), F32),
            vmem((ROW, modes, LANES), F32),
            vmem((ROW, modes, LANES), F32),
            vmem((modes, LANES), F32),
            vmem((ROW + groups * (n_rows + 1), modes, LANES), F32),
            vmem((n_ten, 1, tokens), F32),
            dma(()), dma(()), dma(()), dma(()),
            dma((2,)), dma((groups,)), dma(()), dma(()), dma(()),
            regular, regular, regular,
        ],
        compiler_params=pltpu.CompilerParams(
            collective_id=0, has_side_effects=True, vmem_limit_bytes=32 * 1024 * 1024
        ),
        name="hyena",
    )(*operands)
    return (gated_out * scale).astype(jnp.bfloat16)


def solution(mesh):
    return jax.shard_map(
        body,
        mesh=mesh,
        in_specs=(
            P(TEN, CTX),
            P(TEN, CTX),
            P(TEN, CTX),
            P(TEN, None),
            P(TEN, None),
            P(TEN),
        ),
        out_specs=P(TEN, CTX),
        check_vma=False,
    )
```

```python
import functools

import jax
import jax.numpy as jnp
from jax import lax
from jax.experimental import pallas as pl
from jax.experimental.pallas import tpu as pltpu
from jax.sharding import PartitionSpec as P

MESH = pl.DeviceIdType.MESH
CTX, TEN = "context", "tensor"
LANES = 128
SUB = 32
ROW = 8
LATER_DELEGATE = 7
WIDTH_DELEGATE = 5
GREET_ROW = (2, 3, 1, 4, 5, 6, 7)
SEND_ROW = (6, 7, 5, 4, 3, 2, 1)
ORDER = (
    (1, 0, 0), (1, 1, 0), (2, 0, 0), (2, 1, 0), (3, 0, 0), (3, 1, 0), (1, 0, 1), (1, 1, 1), (2, 0, 1), (2, 1, 1), (3, 0, 1), (3, 1, 1),
)
FAR_WIDTH = (2, 10, 6, 14, 9, 11, 5, 7, 13, 15, 1, 3, 8, 4, 12)
F32 = jnp.float32


def wait_bytes(ref, sem):
    pltpu.make_async_copy(ref, ref, sem).wait()


def kernel(
    n_ctx, n_ten, width,
    q_hbm, k_hbm, v_hbm, res_hbm, rate_hbm, gain_hbm,
    go_ref, scale_ref,
    q_v, kv_v, poles_v, gain_v, go_t,
    g_pad, taps, powers, local, q_t, states, decays,
    across, before, s_buf, a_buf, r_buf, p_out, c_out, arrived, t_buf,
    poles_sem, kv_sem, q_sem, gain_sem, rs1, group_sem, sent_sem, ss3, rs3, row_in, later_in, width_in,
):
    me = lax.axis_index(CTX)
    ten = lax.axis_index(TEN)
    modes = rate_hbm.shape[0]
    chans, tokens = q_hbm.shape
    subs = tokens // SUB
    groups = chans // LANES
    n_rows = n_ctx // ROW
    prefixes = (n_rows - 1) * groups
    half = groups
    row, place = me >> 3, me & (ROW - 1)
    mine = place & (half - 1)
    is_later_delegate = place == LATER_DELEGATE
    is_width_delegate = place == WIDTH_DELEGATE
    beside_delegate = (place == WIDTH_DELEGATE ^ 1) | (place == LATER_DELEGATE ^ 1)
    is_plain = jnp.logical_not(is_later_delegate | is_width_delegate)

    def signal(sem, **where):
        where = {{"ctx": CTX, "ten": TEN}[name]: at for name, at in where.items()}
        pl.semaphore_signal(sem, inc=1, device_id=where, device_id_type=MESH)

    barrier = pltpu.get_barrier_semaphore()
    for step in GREET_ROW:
        other = ((place + step) & (ROW - 1))

        @pl.when((other != LATER_DELEGATE) & (other != WIDTH_DELEGATE))
        def _():
            signal(barrier, ctx=row * ROW + other)

    def greet_earlier(r, carry):
        signal(barrier, ctx=r * ROW + LATER_DELEGATE)
        return carry

    lax.fori_loop(0, row, greet_earlier, 0)

    for src, dst, sem in (
        (rate_hbm, poles_v.at[0], poles_sem), (res_hbm, poles_v.at[1], poles_sem),
        (k_hbm, kv_v.at[0], kv_sem), (v_hbm, kv_v.at[1], kv_sem),
        (q_hbm, q_v, q_sem), (gain_hbm, gain_v, gain_sem),
    ):
        pltpu.make_async_copy(src, dst, sem).start()

    for step in range(1, n_ten):
        signal(barrier, ctx=row * ROW + WIDTH_DELEGATE, ten=(ten + step) & (n_ten - 1))

    g_pad[...] = jnp.zeros_like(g_pad)
    wait_bytes(poles_v, poles_sem)
    rate = poles_v[0]
    decay = jnp.exp(-rate)
    decay_sub = jnp.exp(-SUB * rate)
    wait_bytes(kv_v, kv_sem)
    gated = (kv_v[0].astype(F32) * kv_v[1].astype(F32)).astype(jnp.bfloat16).astype(F32)
    g_pad[:, 8:, :] = gated.T.reshape(subs, SUB, chans)

    def advance(i, hs):
        return tuple(decay * h + g_pad[s, pl.ds(8 + i, 1), :] for s, h in enumerate(hs))

    ends = lax.fori_loop(0, SUB, advance, (jnp.zeros((modes, chans), F32),) * subs, unroll=4)
    state = ends[0]
    states[0] = jnp.zeros((modes, chans), F32)
    for s in range(1, subs):
        states[s] = state
        state = decay_sub * state + ends[s]
    decay_all = jnp.exp(-float(tokens) * rate)

    for g in range(groups):
        s_buf[g] = state[:, LANES * g : LANES * (g + 1)]
        a_buf[g] = decay_all[:, LANES * g : LANES * (g + 1)]

    @pl.when(is_plain)
    def _():
        pl.semaphore_wait(barrier, ROW - 1)

    @pl.when(beside_delegate)
    def _():
        signal(row_in, ctx=row * ROW + (place ^ 1))

    @pl.when(jnp.logical_not(is_plain))
    def _():
        pl.semaphore_wait(row_in, 1)

    for step in SEND_ROW:
        other = ((place + step) & (ROW - 1))
        pltpu.make_async_remote_copy(
            s_buf.at[other & (half - 1)], r_buf.at[place], sent_sem, rs1.at[place >> 2], device_id={CTX: row * ROW + other}, device_id_type=MESH
        ).start()

    from_beside = pltpu.make_async_remote_copy(
        s_buf, arrived.at[pl.ds(prefixes, groups)], sent_sem, rs1.at[0], device_id={CTX: me ^ 1}, device_id_type=MESH
    )

    @pl.when(place == 0)
    def _():
        from_beside.start()

    @pl.when(is_later_delegate)
    def _():
        @pl.when(row < n_rows - 1)
        def _():
            pl.semaphore_wait(barrier, ROW * (n_rows - 1 - row))

        for step in SEND_ROW:
            signal(later_in, ctx=row * ROW + ((place + step) & (ROW - 1)))

    weight = poles_v[1] * jnp.sqrt(rate)
    ages = (lax.broadcasted_iota(jnp.int32, (SUB, chans), 0) + 1).astype(F32)
    total = jnp.zeros((SUB, chans), F32)
    for m in range(modes):
        power = weight[m : m + 1, :] * jnp.exp(-rate[m : m + 1, :] * ages)
        powers[m] = power
        total = total + power
    taps[7:8, :] = jnp.sum(weight, axis=0, keepdims=True)
    taps[8:, :] = total
    for s in range(subs):
        decays[s] = jnp.exp(-float(SUB * s) * rate)

    def convolve(k, carry):
        cols = pl.ds(pl.multiple_of(k * LANES, LANES), LANES)
        acc = [jnp.zeros((subs, 8, LANES), F32) for _ in range(SUB // 8)]
        for shift in range(8):
            pieces = [g_pad[:, pl.ds(8 + 8 * j - shift, 8), cols] for j in range(SUB // 8)]
            for b in range(SUB // 8):
                tap = taps[pl.ds(7 + 8 * b + shift, 1), cols]
                for j in range(b, SUB // 8):
                    acc[j] = acc[j] + tap * pieces[j - b]
        for j in range(SUB // 8):
            local[:, pl.ds(8 * j, 8), cols] = acc[j]
        return carry

    lax.fori_loop(0, groups, convolve, 0)

    r_buf[place] = s_buf[mine]

    ratio = a_buf[mine]

    def scan(held, first):
        for d in range(first, first + half):
            p_out[d] = held
            held = ratio * held + r_buf[d]
        return held

    def give_prefixes():
        for step in range(1, half):
            q = (place & half) + ((place + step) & (half - 1))

            @pl.when(q >= 2)
            def _():
                pltpu.make_async_remote_copy(
                    p_out.at[q], arrived.at[prefixes + mine], sent_sem, group_sem.at[mine],
                    device_id={CTX: row * ROW + q}, device_id_type=MESH,
                ).start()

    for units, here in ((half - 1 + groups, place == 1), (half - 1, (place < half) & (place != 1)), (half, place >= half)):
        @pl.when(here)
        def _():
            wait_bytes(arrived.at[pl.ds(0, units)], rs1.at[0])

    held = scan(jnp.zeros((modes, LANES), F32), 0)

    @pl.when(place < half)
    def _():
        give_prefixes()
        wait_bytes(arrived.at[pl.ds(0, half)], rs1.at[1])

    @pl.when(place >= half)
    def _():
        wait_bytes(arrived.at[pl.ds(0, half - 1)], rs1.at[1])

    c_out[...] = scan(held, half)

    @pl.when(place >= half)
    def _():
        give_prefixes()

    @pl.when(jnp.logical_not(is_later_delegate))
    def _():
        pl.semaphore_wait(later_in, 1)

    for ahead, chip, core in ORDER:
        @pl.when(row + ahead < n_rows)
        def _():
            pltpu.make_async_remote_copy(
                c_out, arrived.at[groups * row + mine], sent_sem, group_sem.at[mine],
                device_id={CTX: (row + ahead) * ROW + (place & half) + 2 * chip + core}, device_id_type=MESH,
            ).start()

    @pl.when(place >= 2)
    def _():
        arrived[prefixes + mine] = p_out[place]

    @pl.when(place == 0)
    def _():
        arrived[prefixes : prefixes + groups] = jnp.zeros((groups, modes, LANES), F32)

    wait_bytes(q_v, q_sem)
    wait_bytes(gain_v, gain_sem)
    q_t[...] = q_v[...].astype(F32).T.reshape(subs, SUB, chans)
    across[...] = jnp.exp(-float(tokens * ROW) * rate)
    before[...] = jnp.exp(-(float(tokens) * place.astype(F32)) * rate)

    @pl.when(is_width_delegate)
    def _():
        pl.semaphore_wait(barrier, ROW * (n_ten - 1))
        for step in SEND_ROW:
            signal(width_in, ctx=row * ROW + ((place + step) & (ROW - 1)))

    def finish(turn, square):
        g = (place & 2) ^ turn
        cols = pl.ds(pl.multiple_of(g * LANES, LANES), LANES)
        count = row + jnp.where((place >= 2) & (g != mine), 1, 0)
        for units in range(1, n_rows + 1):
            @pl.when(count == units)
            def _():
                wait_bytes(arrived.at[pl.ds(0, units)], group_sem.at[g])

        def from_row(r, carried):
            return across[:, cols] * carried + arrived[groups * r + g]

        carried = lax.fori_loop(0, row, from_row, jnp.zeros((modes, LANES), F32))
        start = arrived[prefixes + g] + before[:, cols] * carried
        for s in range(subs):
            states[s, :, cols] = states[s, :, cols] + decays[s, :, cols] * start
        acc = local[:, :, cols]
        for m in range(modes):
            acc = acc + powers[m, :, cols][None] * states[:, pl.ds(m, 1), cols]
        out = q_t[:, :, cols] * acc.astype(jnp.bfloat16).astype(F32)
        go_t[:, :, cols] = out * gain_v[:, cols]
        return square + out * out

    square = lax.fori_loop(0, groups, finish, jnp.zeros((subs, SUB, LANES), F32))

    t_buf[ten] = jnp.sum(square.reshape(tokens, LANES).T, axis=0, keepdims=True)

    @pl.when(jnp.logical_not(is_width_delegate))
    def _():
        pl.semaphore_wait(width_in, 1)

    for step in FAR_WIDTH:
        pltpu.make_async_remote_copy(
            t_buf.at[ten], t_buf.at[ten], ss3, rs3,
            device_id={TEN: ((ten + step) & (n_ten - 1))}, device_id_type=MESH,
        ).start()

    go_ref[...] = go_t[...].reshape(tokens, chans).T

    for r in range(n_rows):
        for first, last, prefix_units in ((0, 0, groups + 2), (1, 1, 2), (2, 3, 1), (4, 7, 3)):
            @pl.when((row == r) & (place >= first) & (place <= last))
            def _():
                wait_bytes(arrived.at[pl.ds(0, ROW - 1 + prefix_units + half * (n_rows - 1 - r))], sent_sem)

    wait_bytes(t_buf.at[pl.ds(0, n_ten - 1)], ss3)
    wait_bytes(t_buf.at[pl.ds(0, n_ten - 1)], rs3)
    scale_ref[...] = lax.rsqrt(jnp.sum(t_buf[...], axis=0) / width + 1e-05)


def body(q_gate, k_gate, values, residues, rates, gain):
    n_ctx, n_ten = lax.axis_size(CTX), lax.axis_size(TEN)
    chans, tokens = q_gate.shape
    modes = rates.shape[1]
    subs, groups, n_rows = tokens // SUB, chans // LANES, n_ctx // ROW
    vmem, dma, regular = pltpu.VMEM, pltpu.SemaphoreType.DMA, pltpu.SemaphoreType.REGULAR
    operands = (q_gate, k_gate, values, residues.T, rates.T, gain.reshape(1, chans))
    operands = [pltpu.with_memory_space_constraint(x, pltpu.HBM) for x in operands]
    gated_out, scale = pl.pallas_call(
        functools.partial(kernel, n_ctx, n_ten, float(chans * n_ten)),
        out_shape=(
            vmem((chans, tokens), F32),
            vmem((1, tokens), F32),
        ),
        in_specs=[pl.BlockSpec(memory_space=pltpu.HBM)] * 6,
        out_specs=(pl.BlockSpec(memory_space=pltpu.VMEM), pl.BlockSpec(memory_space=pltpu.VMEM)),
        scratch_shapes=[
            vmem((chans, tokens), jnp.bfloat16),
            vmem((2, chans, tokens), jnp.bfloat16),
            vmem((2, modes, chans), F32),
            vmem((1, chans), F32),
            vmem((subs, SUB, chans), F32),
            vmem((subs, 8 + SUB, chans), F32),
            vmem((8 + SUB, chans), F32),
            vmem((modes, SUB, chans), F32),
            vmem((subs, SUB, chans), F32),
            vmem((subs, SUB, chans), F32),
            vmem((subs, modes, chans), F32),
            vmem((subs, modes, chans), F32),
            vmem((modes, chans), F32),
            vmem((modes, chans), F32),
            vmem((groups, modes, LANES), F32),
            vmem((groups, modes, LANES), F32),
            vmem((ROW, modes, LANES), F32),
            vmem((ROW, modes, LANES), F32),
            vmem((modes, LANES), F32),
            vmem((ROW + groups * (n_rows + 1), modes, LANES), F32),
            vmem((n_ten, 1, tokens), F32),
            dma(()), dma(()), dma(()), dma(()),
            dma((2,)), dma((groups,)), dma(()), dma(()), dma(()),
            regular, regular, regular,
        ],
        compiler_params=pltpu.CompilerParams(
            collective_id=0, has_side_effects=True, vmem_limit_bytes=32 * 1024 * 1024
        ),
        name="hyena",
    )(*operands)
    return (gated_out * scale).astype(jnp.bfloat16)


def solution(mesh):
    return jax.shard_map(
        body,
        mesh=mesh,
        in_specs=(
            P(TEN, CTX),
            P(TEN, CTX),
            P(TEN, CTX),
            P(TEN, None),
            P(TEN, None),
            P(TEN),
        ),
        out_specs=P(TEN, CTX),
        check_vma=False,
    )
```

```python
import functools

import jax
import jax.numpy as jnp
from jax import lax
from jax.experimental import pallas as pl
from jax.experimental.pallas import tpu as pltpu
from jax.sharding import PartitionSpec as P

MESH = pl.DeviceIdType.MESH
CTX, TEN = "context", "tensor"
LANES = 128
SUB = 32
ROW = 8
LATER_DELEGATE = 7
WIDTH_DELEGATE = 5
GREET_ROW = (2, 3, 1, 4, 5, 6, 7)
SEND_ROW = (6, 7, 5, 4, 3, 2, 1)
ORDER = (
    (1, 0, 0), (1, 1, 0), (2, 0, 0), (2, 1, 0), (3, 0, 0), (3, 1, 0), (1, 0, 1), (1, 1, 1), (2, 0, 1), (2, 1, 1), (3, 0, 1), (3, 1, 1),
)
FAR_WIDTH = (2, 10, 6, 14, 9, 11, 5, 7, 13, 15, 1, 3, 8, 4, 12)
F32 = jnp.float32


def wait_bytes(ref, sem):
    pltpu.make_async_copy(ref, ref, sem).wait()


def kernel(
    n_ctx, n_ten, width,
    q_hbm, k_hbm, v_hbm, res_hbm, rate_hbm, gain_hbm,
    go_ref, scale_ref,
    q_v, kv_v, poles_v, gain_v, go_t,
    g_pad, taps, powers, local, q_t, states, decays,
    across, before, s_buf, a_buf, r_buf, p_out, c_out, arrived, t_buf,
    poles_sem, kv_sem, q_sem, gain_sem, rs1, group_sem, sent_sem, ss3, rs3, later_in, width_in,
):
    me = lax.axis_index(CTX)
    ten = lax.axis_index(TEN)
    modes = rate_hbm.shape[0]
    chans, tokens = q_hbm.shape
    subs = tokens // SUB
    groups = chans // LANES
    n_rows = n_ctx // ROW
    prefixes = (n_rows - 1) * groups
    half = groups
    row, place = me >> 3, me & (ROW - 1)
    mine = place & (half - 1)
    is_later_delegate = place == LATER_DELEGATE
    is_width_delegate = place == WIDTH_DELEGATE
    beside_delegate = (place == WIDTH_DELEGATE ^ 1) | (place == LATER_DELEGATE ^ 1)
    is_plain = jnp.logical_not(is_later_delegate | is_width_delegate)

    def signal(sem, **where):
        where = {{"ctx": CTX, "ten": TEN}[name]: at for name, at in where.items()}
        pl.semaphore_signal(sem, inc=1, device_id=where, device_id_type=MESH)

    barrier = pltpu.get_barrier_semaphore()
    for step in GREET_ROW:
        other = ((place + step) & (ROW - 1))

        @pl.when((other != LATER_DELEGATE) & (other != WIDTH_DELEGATE))
        def _():
            signal(barrier, ctx=row * ROW + other)

    def greet_earlier(r, carry):
        signal(barrier, ctx=r * ROW + LATER_DELEGATE)
        return carry

    lax.fori_loop(0, row, greet_earlier, 0)

    for src, dst, sem in (
        (rate_hbm, poles_v.at[0], poles_sem), (res_hbm, poles_v.at[1], poles_sem),
        (k_hbm, kv_v.at[0], kv_sem), (v_hbm, kv_v.at[1], kv_sem),
        (q_hbm, q_v, q_sem), (gain_hbm, gain_v, gain_sem),
    ):
        pltpu.make_async_copy(src, dst, sem).start()

    for step in range(1, n_ten):
        signal(barrier, ctx=row * ROW + WIDTH_DELEGATE, ten=(ten + step) & (n_ten - 1))

    g_pad[...] = jnp.zeros_like(g_pad)
    wait_bytes(poles_v, poles_sem)
    rate = poles_v[0]
    decay = jnp.exp(-rate)
    decay_sub = jnp.exp(-SUB * rate)
    wait_bytes(kv_v, kv_sem)
    gated = (kv_v[0].astype(F32) * kv_v[1].astype(F32)).astype(jnp.bfloat16).astype(F32)
    g_pad[:, 8:, :] = gated.T.reshape(subs, SUB, chans)

    def advance(i, hs):
        return tuple(decay * h + g_pad[s, pl.ds(8 + i, 1), :] for s, h in enumerate(hs))

    ends = lax.fori_loop(0, SUB, advance, (jnp.zeros((modes, chans), F32),) * subs, unroll=32)
    state = ends[0]
    states[0] = jnp.zeros((modes, chans), F32)
    for s in range(1, subs):
        states[s] = state
        state = decay_sub * state + ends[s]
    decay_all = jnp.exp(-float(tokens) * rate)

    for g in range(groups):
        s_buf[g] = state[:, LANES * g : LANES * (g + 1)]
        a_buf[g] = decay_all[:, LANES * g : LANES * (g + 1)]

    @pl.when(is_plain)
    def _():
        pl.semaphore_wait(barrier, ROW - 1)

    @pl.when(place == WIDTH_DELEGATE ^ 1)
    def _():
        signal(width_in, ctx=row * ROW + WIDTH_DELEGATE)

    @pl.when(place == LATER_DELEGATE ^ 1)
    def _():
        signal(later_in, ctx=row * ROW + LATER_DELEGATE)

    @pl.when(is_width_delegate)
    def _():
        pl.semaphore_wait(width_in, 1)

    @pl.when(is_later_delegate)
    def _():
        pl.semaphore_wait(later_in, 1)

    for step in SEND_ROW:
        other = ((place + step) & (ROW - 1))
        pltpu.make_async_remote_copy(
            s_buf.at[other & (half - 1)], r_buf.at[place], sent_sem, rs1.at[place >> 2], device_id={CTX: row * ROW + other}, device_id_type=MESH
        ).start()

    from_beside = pltpu.make_async_remote_copy(
        s_buf, arrived.at[pl.ds(prefixes, groups)], sent_sem, rs1.at[0], device_id={CTX: me ^ 1}, device_id_type=MESH
    )

    @pl.when(place == 0)
    def _():
        from_beside.start()

    @pl.when(is_later_delegate)
    def _():
        @pl.when(row < n_rows - 1)
        def _():
            pl.semaphore_wait(barrier, ROW * (n_rows - 1 - row))

        for step in SEND_ROW:
            signal(later_in, ctx=row * ROW + ((place + step) & (ROW - 1)))

    weight = poles_v[1] * jnp.sqrt(rate)
    ages = (lax.broadcasted_iota(jnp.int32, (SUB, chans), 0) + 1).astype(F32)
    total = jnp.zeros((SUB, chans), F32)
    for m in range(modes):
        power = weight[m : m + 1, :] * jnp.exp(-rate[m : m + 1, :] * ages)
        powers[m] = power
        total = total + power
    taps[7:8, :] = jnp.sum(weight, axis=0, keepdims=True)
    taps[8:, :] = total
    for s in range(subs):
        decays[s] = jnp.exp(-float(SUB * s) * rate)

    def convolve(k, carry):
        cols = pl.ds(pl.multiple_of(k * LANES, LANES), LANES)
        acc = [jnp.zeros((subs, 8, LANES), F32) for _ in range(SUB // 8)]
        for shift in range(8):
            pieces = [g_pad[:, pl.ds(8 + 8 * j - shift, 8), cols] for j in range(SUB // 8)]
            for b in range(SUB // 8):
                tap = taps[pl.ds(7 + 8 * b + shift, 1), cols]
                for j in range(b, SUB // 8):
                    acc[j] = acc[j] + tap * pieces[j - b]
        for j in range(SUB // 8):
            local[:, pl.ds(8 * j, 8), cols] = acc[j]
        return carry

    lax.fori_loop(0, groups, convolve, 0)

    r_buf[place] = s_buf[mine]

    ratio = a_buf[mine]

    def scan(held, first):
        for d in range(first, first + half):
            p_out[d] = held
            held = ratio * held + r_buf[d]
        return held

    def give_prefixes():
        for step in range(1, half):
            q = (place & half) + ((place + step) & (half - 1))

            @pl.when(q >= 2)
            def _():
                pltpu.make_async_remote_copy(
                    p_out.at[q], arrived.at[prefixes + mine], sent_sem, group_sem.at[mine],
                    device_id={CTX: row * ROW + q}, device_id_type=MESH,
                ).start()

    for units, here in ((half - 1 + groups, place == 1), (half - 1, (place < half) & (place != 1)), (half, place >= half)):
        @pl.when(here)
        def _():
            wait_bytes(arrived.at[pl.ds(0, units)], rs1.at[0])

    held = scan(jnp.zeros((modes, LANES), F32), 0)

    @pl.when(place < half)
    def _():
        give_prefixes()
        wait_bytes(arrived.at[pl.ds(0, half)], rs1.at[1])

    @pl.when(place >= half)
    def _():
        wait_bytes(arrived.at[pl.ds(0, half - 1)], rs1.at[1])

    c_out[...] = scan(held, half)

    @pl.when(place >= half)
    def _():
        give_prefixes()

    @pl.when(jnp.logical_not(is_later_delegate))
    def _():
        pl.semaphore_wait(later_in, 1)

    for ahead, chip, core in ORDER:
        @pl.when(row + ahead < n_rows)
        def _():
            pltpu.make_async_remote_copy(
                c_out, arrived.at[groups * row + mine], sent_sem, group_sem.at[mine],
                device_id={CTX: (row + ahead) * ROW + (place & half) + 2 * chip + core}, device_id_type=MESH,
            ).start()

    @pl.when(place >= 2)
    def _():
        arrived[prefixes + mine] = p_out[place]

    @pl.when(place == 0)
    def _():
        arrived[prefixes : prefixes + groups] = jnp.zeros((groups, modes, LANES), F32)

    wait_bytes(q_v, q_sem)
    wait_bytes(gain_v, gain_sem)
    q_t[...] = q_v[...].astype(F32).T.reshape(subs, SUB, chans)
    across[...] = jnp.exp(-float(tokens * ROW) * rate)
    before[...] = jnp.exp(-(float(tokens) * place.astype(F32)) * rate)

    @pl.when(is_width_delegate)
    def _():
        pl.semaphore_wait(barrier, ROW * (n_ten - 1))
        for step in SEND_ROW:
            signal(width_in, ctx=row * ROW + ((place + step) & (ROW - 1)))

    def finish(turn, square):
        g = (place & 2) ^ turn
        cols = pl.ds(pl.multiple_of(g * LANES, LANES), LANES)
        count = row + jnp.where((place >= 2) & (g != mine), 1, 0)
        for units in range(1, n_rows + 1):
            @pl.when(count == units)
            def _():
                wait_bytes(arrived.at[pl.ds(0, units)], group_sem.at[g])

        def from_row(r, carried):
            return across[:, cols] * carried + arrived[groups * r + g]

        carried = lax.fori_loop(0, row, from_row, jnp.zeros((modes, LANES), F32))
        start = arrived[prefixes + g] + before[:, cols] * carried
        for s in range(subs):
            states[s, :, cols] = states[s, :, cols] + decays[s, :, cols] * start
        acc = local[:, :, cols]
        for m in range(modes):
            acc = acc + powers[m, :, cols][None] * states[:, pl.ds(m, 1), cols]
        out = q_t[:, :, cols] * acc.astype(jnp.bfloat16).astype(F32)
        go_t[:, :, cols] = out * gain_v[:, cols]
        return square + out * out

    square = lax.fori_loop(0, groups, finish, jnp.zeros((subs, SUB, LANES), F32))

    t_buf[ten] = jnp.sum(square.reshape(tokens, LANES).T, axis=0, keepdims=True)

    @pl.when(jnp.logical_not(is_width_delegate))
    def _():
        pl.semaphore_wait(width_in, 1)

    for step in FAR_WIDTH:
        pltpu.make_async_remote_copy(
            t_buf.at[ten], t_buf.at[ten], ss3, rs3,
            device_id={TEN: ((ten + step) & (n_ten - 1))}, device_id_type=MESH,
        ).start()

    go_ref[...] = go_t[...].reshape(tokens, chans).T

    for r in range(n_rows):
        for first, last, prefix_units in ((0, 0, groups + 2), (1, 1, 2), (2, 3, 1), (4, 7, 3)):
            @pl.when((row == r) & (place >= first) & (place <= last))
            def _():
                wait_bytes(arrived.at[pl.ds(0, ROW - 1 + prefix_units + half * (n_rows - 1 - r))], sent_sem)

    wait_bytes(t_buf.at[pl.ds(0, n_ten - 1)], ss3)
    wait_bytes(t_buf.at[pl.ds(0, n_ten - 1)], rs3)
    scale_ref[...] = lax.rsqrt(jnp.sum(t_buf[...], axis=0) / width + 1e-05)


def body(q_gate, k_gate, values, residues, rates, gain):
    n_ctx, n_ten = lax.axis_size(CTX), lax.axis_size(TEN)
    chans, tokens = q_gate.shape
    modes = rates.shape[1]
    subs, groups, n_rows = tokens // SUB, chans // LANES, n_ctx // ROW
    vmem, dma, regular = pltpu.VMEM, pltpu.SemaphoreType.DMA, pltpu.SemaphoreType.REGULAR
    operands = (q_gate, k_gate, values, residues.T, rates.T, gain.reshape(1, chans))
    operands = [pltpu.with_memory_space_constraint(x, pltpu.HBM) for x in operands]
    gated_out, scale = pl.pallas_call(
        functools.partial(kernel, n_ctx, n_ten, float(chans * n_ten)),
        out_shape=(
            vmem((chans, tokens), F32),
            vmem((1, tokens), F32),
        ),
        in_specs=[pl.BlockSpec(memory_space=pltpu.HBM)] * 6,
        out_specs=(pl.BlockSpec(memory_space=pltpu.VMEM), pl.BlockSpec(memory_space=pltpu.VMEM)),
        scratch_shapes=[
            vmem((chans, tokens), jnp.bfloat16),
            vmem((2, chans, tokens), jnp.bfloat16),
            vmem((2, modes, chans), F32),
            vmem((1, chans), F32),
            vmem((subs, SUB, chans), F32),
            vmem((subs, 8 + SUB, chans), F32),
            vmem((8 + SUB, chans), F32),
            vmem((modes, SUB, chans), F32),
            vmem((subs, SUB, chans), F32),
            vmem((subs, SUB, chans), F32),
            vmem((subs, modes, chans), F32),
            vmem((subs, modes, chans), F32),
            vmem((modes, chans), F32),
            vmem((modes, chans), F32),
            vmem((groups, modes, LANES), F32),
            vmem((groups, modes, LANES), F32),
            vmem((ROW, modes, LANES), F32),
            vmem((ROW, modes, LANES), F32),
            vmem((modes, LANES), F32),
            vmem((ROW + groups * (n_rows + 1), modes, LANES), F32),
            vmem((n_ten, 1, tokens), F32),
            dma(()), dma(()), dma(()), dma(()),
            dma((2,)), dma((groups,)), dma(()), dma(()), dma(()),
            regular, regular,
        ],
        compiler_params=pltpu.CompilerParams(
            collective_id=0, has_side_effects=True, vmem_limit_bytes=32 * 1024 * 1024
        ),
        name="hyena",
    )(*operands)
    return (gated_out * scale).astype(jnp.bfloat16)


def solution(mesh):
    return jax.shard_map(
        body,
        mesh=mesh,
        in_specs=(
            P(TEN, CTX),
            P(TEN, CTX),
            P(TEN, CTX),
            P(TEN, None),
            P(TEN, None),
            P(TEN),
        ),
        out_specs=P(TEN, CTX),
        check_vma=False,
    )
```

```python
import functools

import jax
import jax.numpy as jnp
from jax import lax
from jax.experimental import pallas as pl
from jax.experimental.pallas import tpu as pltpu
from jax.sharding import PartitionSpec as P

MESH = pl.DeviceIdType.MESH
CTX, TEN = "context", "tensor"
LANES = 128
SUB = 32
ROW = 8
LATER_DELEGATE = 7
WIDTH_DELEGATE = 5
GREET_ROW = (2, 3, 1, 4, 5, 6, 7)
SEND_ROW = (6, 7, 5, 4, 3, 2, 1)
ORDER = (
    (1, 0, 0), (1, 1, 0), (2, 0, 0), (2, 1, 0), (3, 0, 0), (3, 1, 0), (1, 0, 1), (1, 1, 1), (2, 0, 1), (2, 1, 1), (3, 0, 1), (3, 1, 1),
)
FAR_WIDTH = (2, 10, 6, 14, 9, 11, 5, 7, 13, 15, 1, 3, 8, 4, 12)
F32 = jnp.float32


def wait_bytes(ref, sem):
    pltpu.make_async_copy(ref, ref, sem).wait()


def kernel(
    n_ctx, n_ten, width,
    q_hbm, k_hbm, v_hbm, res_hbm, rate_hbm, gain_hbm,
    go_ref, scale_ref,
    q_v, kv_v, poles_v, gain_v, go_t,
    g_pad, taps, powers, local, q_t, states, decays,
    across, before, s_buf, a_buf, r_buf, p_out, c_out, arrived, t_buf,
    poles_sem, kv_sem, q_sem, gain_sem, rs1, chip_sem, sent_sem, ss3, rs3, later_in, width_in,
):
    me = lax.axis_index(CTX)
    ten = lax.axis_index(TEN)
    modes = rate_hbm.shape[0]
    chans, tokens = q_hbm.shape
    subs = tokens // SUB
    groups = chans // LANES
    n_rows = n_ctx // ROW
    prefixes = (n_rows - 1) * groups
    half = groups
    row, place = me >> 3, me & (ROW - 1)
    mine = place & (half - 1)
    is_later_delegate = place == LATER_DELEGATE
    is_width_delegate = place == WIDTH_DELEGATE
    beside_delegate = (place == WIDTH_DELEGATE ^ 1) | (place == LATER_DELEGATE ^ 1)
    is_plain = jnp.logical_not(is_later_delegate | is_width_delegate)

    def signal(sem, **where):
        where = {{"ctx": CTX, "ten": TEN}[name]: at for name, at in where.items()}
        pl.semaphore_signal(sem, inc=1, device_id=where, device_id_type=MESH)

    barrier = pltpu.get_barrier_semaphore()
    for step in GREET_ROW:
        other = ((place + step) & (ROW - 1))

        @pl.when((other != LATER_DELEGATE) & (other != WIDTH_DELEGATE))
        def _():
            signal(barrier, ctx=row * ROW + other)

    def greet_earlier(r, carry):
        signal(barrier, ctx=r * ROW + LATER_DELEGATE)
        return carry

    lax.fori_loop(0, row, greet_earlier, 0)

    for src, dst, sem in (
        (rate_hbm, poles_v.at[0], poles_sem), (res_hbm, poles_v.at[1], poles_sem),
        (k_hbm, kv_v.at[0], kv_sem), (v_hbm, kv_v.at[1], kv_sem),
        (q_hbm, q_v, q_sem), (gain_hbm, gain_v, gain_sem),
    ):
        pltpu.make_async_copy(src, dst, sem).start()

    for step in range(1, n_ten):
        signal(barrier, ctx=row * ROW + WIDTH_DELEGATE, ten=(ten + step) & (n_ten - 1))

    g_pad[...] = jnp.zeros_like(g_pad)
    wait_bytes(poles_v, poles_sem)
    rate = poles_v[0]
    decay = jnp.exp(-rate)
    decay_sub = jnp.exp(-SUB * rate)
    wait_bytes(kv_v, kv_sem)
    gated = (kv_v[0].astype(F32) * kv_v[1].astype(F32)).astype(jnp.bfloat16).astype(F32)
    g_pad[:, 8:, :] = gated.T.reshape(subs, SUB, chans)

    def advance(i, hs):
        return tuple(decay * h + g_pad[s, pl.ds(8 + i, 1), :] for s, h in enumerate(hs))

    ends = lax.fori_loop(0, SUB, advance, (jnp.zeros((modes, chans), F32),) * subs, unroll=32)
    state = ends[0]
    states[0] = jnp.zeros((modes, chans), F32)
    for s in range(1, subs):
        states[s] = state
        state = decay_sub * state + ends[s]
    decay_all = jnp.exp(-float(tokens) * rate)

    for g in range(groups):
        s_buf[g] = state[:, LANES * g : LANES * (g + 1)]
        a_buf[g] = decay_all[:, LANES * g : LANES * (g + 1)]

    @pl.when(is_plain)
    def _():
        pl.semaphore_wait(barrier, ROW - 1)

    @pl.when(place == WIDTH_DELEGATE ^ 1)
    def _():
        signal(width_in, ctx=row * ROW + WIDTH_DELEGATE)

    @pl.when(place == LATER_DELEGATE ^ 1)
    def _():
        signal(later_in, ctx=row * ROW + LATER_DELEGATE)

    @pl.when(is_width_delegate)
    def _():
        pl.semaphore_wait(width_in, 1)

    @pl.when(is_later_delegate)
    def _():
        pl.semaphore_wait(later_in, 1)

    for step in SEND_ROW:
        other = ((place + step) & (ROW - 1))
        pltpu.make_async_remote_copy(
            s_buf.at[other & (half - 1)], r_buf.at[place], sent_sem, rs1.at[place >> 2], device_id={CTX: row * ROW + other}, device_id_type=MESH
        ).start()

    from_beside = pltpu.make_async_remote_copy(
        s_buf, arrived.at[pl.ds(prefixes, groups)], sent_sem, rs1.at[0], device_id={CTX: me ^ 1}, device_id_type=MESH
    )

    @pl.when(place == 0)
    def _():
        from_beside.start()

    @pl.when(is_later_delegate)
    def _():
        @pl.when(row < n_rows - 1)
        def _():
            pl.semaphore_wait(barrier, ROW * (n_rows - 1 - row))

        for step in SEND_ROW:
            signal(later_in, ctx=row * ROW + ((place + step) & (ROW - 1)))

    weight = poles_v[1] * jnp.sqrt(rate)
    ages = (lax.broadcasted_iota(jnp.int32, (SUB, chans), 0) + 1).astype(F32)
    total = jnp.zeros((SUB, chans), F32)
    for m in range(modes):
        power = weight[m : m + 1, :] * jnp.exp(-rate[m : m + 1, :] * ages)
        powers[m] = power
        total = total + power
    taps[7:8, :] = jnp.sum(weight, axis=0, keepdims=True)
    taps[8:, :] = total
    for s in range(subs):
        decays[s] = jnp.exp(-float(SUB * s) * rate)

    def convolve(k, carry):
        cols = pl.ds(pl.multiple_of(k * LANES, LANES), LANES)
        acc = [jnp.zeros((subs, 8, LANES), F32) for _ in range(SUB // 8)]
        for shift in range(8):
            pieces = [g_pad[:, pl.ds(8 + 8 * j - shift, 8), cols] for j in range(SUB // 8)]
            for b in range(SUB // 8):
                tap = taps[pl.ds(7 + 8 * b + shift, 1), cols]
                for j in range(b, SUB // 8):
                    acc[j] = acc[j] + tap * pieces[j - b]
        for j in range(SUB // 8):
            local[:, pl.ds(8 * j, 8), cols] = acc[j]
        return carry

    lax.fori_loop(0, groups, convolve, 0)

    r_buf[place] = s_buf[mine]

    ratio = a_buf[mine]

    def scan(held, first):
        for d in range(first, first + half):
            p_out[d] = held
            held = ratio * held + r_buf[d]
        return held

    def give_prefixes():
        for step in range(1, half):
            q = (place & half) + ((place + step) & (half - 1))

            @pl.when(q >= 2)
            def _():
                pltpu.make_async_remote_copy(
                    p_out.at[q], arrived.at[prefixes + mine], sent_sem, chip_sem.at[mine >> 1],
                    device_id={CTX: row * ROW + q}, device_id_type=MESH,
                ).start()

    for units, here in ((half - 1 + groups, place == 1), (half - 1, (place < half) & (place != 1)), (half, place >= half)):
        @pl.when(here)
        def _():
            wait_bytes(arrived.at[pl.ds(0, units)], rs1.at[0])

    held = scan(jnp.zeros((modes, LANES), F32), 0)

    @pl.when(place < half)
    def _():
        give_prefixes()
        wait_bytes(arrived.at[pl.ds(0, half)], rs1.at[1])

    @pl.when(place >= half)
    def _():
        wait_bytes(arrived.at[pl.ds(0, half - 1)], rs1.at[1])

    c_out[...] = scan(held, half)

    @pl.when(place >= half)
    def _():
        give_prefixes()

    @pl.when(jnp.logical_not(is_later_delegate))
    def _():
        pl.semaphore_wait(later_in, 1)

    for ahead, chip, core in ORDER:
        @pl.when(row + ahead < n_rows)
        def _():
            pltpu.make_async_remote_copy(
                c_out, arrived.at[groups * row + mine], sent_sem, chip_sem.at[mine >> 1],
                device_id={CTX: (row + ahead) * ROW + (place & half) + 2 * chip + core}, device_id_type=MESH,
            ).start()

    @pl.when(place >= 2)
    def _():
        arrived[prefixes + mine] = p_out[place]

    @pl.when(place == 0)
    def _():
        arrived[prefixes : prefixes + groups] = jnp.zeros((groups, modes, LANES), F32)

    wait_bytes(q_v, q_sem)
    wait_bytes(gain_v, gain_sem)
    q_t[...] = q_v[...].astype(F32).T.reshape(subs, SUB, chans)
    across[...] = jnp.exp(-float(tokens * ROW) * rate)
    before[...] = jnp.exp(-(float(tokens) * place.astype(F32)) * rate)

    @pl.when(is_width_delegate)
    def _():
        pl.semaphore_wait(barrier, ROW * (n_ten - 1))
        for step in SEND_ROW:
            signal(width_in, ctx=row * ROW + ((place + step) & (ROW - 1)))

    def finish(turn, square):
        g = (place & 2) ^ turn
        cols = pl.ds(pl.multiple_of(g * LANES, LANES), LANES)

        count = 2 * row + jnp.where(place < 2, 0, jnp.where(turn < 2, 1, 2))
        for units in range(1, 2 * n_rows + 1):
            @pl.when((count == units) & (turn % 2 == 0))
            def _():
                wait_bytes(arrived.at[pl.ds(0, units)], chip_sem.at[g >> 1])

        def from_row(r, carried):
            return across[:, cols] * carried + arrived[groups * r + g]

        carried = lax.fori_loop(0, row, from_row, jnp.zeros((modes, LANES), F32))
        start = arrived[prefixes + g] + before[:, cols] * carried
        for s in range(subs):
            states[s, :, cols] = states[s, :, cols] + decays[s, :, cols] * start
        acc = local[:, :, cols]
        for m in range(modes):
            acc = acc + powers[m, :, cols][None] * states[:, pl.ds(m, 1), cols]
        out = q_t[:, :, cols] * acc.astype(jnp.bfloat16).astype(F32)
        go_t[:, :, cols] = out * gain_v[:, cols]
        return square + out * out

    square = lax.fori_loop(0, groups, finish, jnp.zeros((subs, SUB, LANES), F32))

    t_buf[ten] = jnp.sum(square.reshape(tokens, LANES).T, axis=0, keepdims=True)

    @pl.when(jnp.logical_not(is_width_delegate))
    def _():
        pl.semaphore_wait(width_in, 1)

    for step in FAR_WIDTH:
        pltpu.make_async_remote_copy(
            t_buf.at[ten], t_buf.at[ten], ss3, rs3,
            device_id={TEN: ((ten + step) & (n_ten - 1))}, device_id_type=MESH,
        ).start()

    go_ref[...] = go_t[...].reshape(tokens, chans).T

    for r in range(n_rows):
        for first, last, prefix_units in ((0, 0, groups + 2), (1, 1, 2), (2, 3, 1), (4, 7, 3)):
            @pl.when((row == r) & (place >= first) & (place <= last))
            def _():
                wait_bytes(arrived.at[pl.ds(0, ROW - 1 + prefix_units + half * (n_rows - 1 - r))], sent_sem)

    wait_bytes(t_buf.at[pl.ds(0, n_ten - 1)], ss3)
    wait_bytes(t_buf.at[pl.ds(0, n_ten - 1)], rs3)
    scale_ref[...] = lax.rsqrt(jnp.sum(t_buf[...], axis=0) / width + 1e-05)


def body(q_gate, k_gate, values, residues, rates, gain):
    n_ctx, n_ten = lax.axis_size(CTX), lax.axis_size(TEN)
    chans, tokens = q_gate.shape
    modes = rates.shape[1]
    subs, groups, n_rows = tokens // SUB, chans // LANES, n_ctx // ROW
    vmem, dma, regular = pltpu.VMEM, pltpu.SemaphoreType.DMA, pltpu.SemaphoreType.REGULAR
    operands = (q_gate, k_gate, values, residues.T, rates.T, gain.reshape(1, chans))
    operands = [pltpu.with_memory_space_constraint(x, pltpu.HBM) for x in operands]
    gated_out, scale = pl.pallas_call(
        functools.partial(kernel, n_ctx, n_ten, float(chans * n_ten)),
        out_shape=(
            vmem((chans, tokens), F32),
            vmem((1, tokens), F32),
        ),
        in_specs=[pl.BlockSpec(memory_space=pltpu.HBM)] * 6,
        out_specs=(pl.BlockSpec(memory_space=pltpu.VMEM), pl.BlockSpec(memory_space=pltpu.VMEM)),
        scratch_shapes=[
            vmem((chans, tokens), jnp.bfloat16),
            vmem((2, chans, tokens), jnp.bfloat16),
            vmem((2, modes, chans), F32),
            vmem((1, chans), F32),
            vmem((subs, SUB, chans), F32),
            vmem((subs, 8 + SUB, chans), F32),
            vmem((8 + SUB, chans), F32),
            vmem((modes, SUB, chans), F32),
            vmem((subs, SUB, chans), F32),
            vmem((subs, SUB, chans), F32),
            vmem((subs, modes, chans), F32),
            vmem((subs, modes, chans), F32),
            vmem((modes, chans), F32),
            vmem((modes, chans), F32),
            vmem((groups, modes, LANES), F32),
            vmem((groups, modes, LANES), F32),
            vmem((ROW, modes, LANES), F32),
            vmem((ROW, modes, LANES), F32),
            vmem((modes, LANES), F32),
            vmem((ROW + groups * (n_rows + 1), modes, LANES), F32),
            vmem((n_ten, 1, tokens), F32),
            dma(()), dma(()), dma(()), dma(()),
            dma((2,)), dma((2,)), dma(()), dma(()), dma(()),
            regular, regular,
        ],
        compiler_params=pltpu.CompilerParams(
            collective_id=0, has_side_effects=True, vmem_limit_bytes=32 * 1024 * 1024
        ),
        name="hyena",
    )(*operands)
    return (gated_out * scale).astype(jnp.bfloat16)


def solution(mesh):
    return jax.shard_map(
        body,
        mesh=mesh,
        in_specs=(
            P(TEN, CTX),
            P(TEN, CTX),
            P(TEN, CTX),
            P(TEN, None),
            P(TEN, None),
            P(TEN),
        ),
        out_specs=P(TEN, CTX),
        check_vma=False,
    )
```

```python
import functools

import jax
import jax.numpy as jnp
from jax import lax
from jax.experimental import pallas as pl
from jax.experimental.pallas import tpu as pltpu
from jax.sharding import PartitionSpec as P

MESH = pl.DeviceIdType.MESH
CTX, TEN = "context", "tensor"
LANES = 128
SUB = 32
ROW = 8
LATER_DELEGATE = 7
WIDTH_DELEGATE = 5
GREET_ROW = (2, 3, 1, 4, 5, 6, 7)
SEND_ROW = (6, 7, 5, 4, 3, 2, 1)
ORDER = (
    (1, 0, 0), (1, 1, 0), (2, 0, 0), (2, 1, 0), (3, 0, 0), (1, 0, 1), (3, 1, 0), (1, 1, 1), (2, 0, 1), (2, 1, 1), (3, 0, 1), (3, 1, 1),
)
FAR_WIDTH = (2, 10, 6, 14, 9, 11, 5, 7, 13, 15, 1, 3, 8, 4, 12)
F32 = jnp.float32


def wait_bytes(ref, sem):
    pltpu.make_async_copy(ref, ref, sem).wait()


def kernel(
    n_ctx, n_ten, width,
    q_hbm, k_hbm, v_hbm, res_hbm, rate_hbm, gain_hbm,
    go_ref, scale_ref,
    q_v, kv_v, poles_v, gain_v, go_t,
    g_pad, taps, powers, local, q_t, states, decays,
    across, before, s_buf, a_buf, r_buf, p_out, c_out, arrived, t_buf,
    poles_sem, kv_sem, q_sem, gain_sem, rs1, chip_sem, sent_sem, ss3, rs3, later_in, width_in,
):
    me = lax.axis_index(CTX)
    ten = lax.axis_index(TEN)
    modes = rate_hbm.shape[0]
    chans, tokens = q_hbm.shape
    subs = tokens // SUB
    groups = chans // LANES
    n_rows = n_ctx // ROW
    prefixes = (n_rows - 1) * groups
    half = groups
    row, place = me >> 3, me & (ROW - 1)
    mine = place & (half - 1)
    is_later_delegate = place == LATER_DELEGATE
    is_width_delegate = place == WIDTH_DELEGATE
    beside_delegate = (place == WIDTH_DELEGATE ^ 1) | (place == LATER_DELEGATE ^ 1)
    is_plain = jnp.logical_not(is_later_delegate | is_width_delegate)

    def signal(sem, **where):
        where = {{"ctx": CTX, "ten": TEN}[name]: at for name, at in where.items()}
        pl.semaphore_signal(sem, inc=1, device_id=where, device_id_type=MESH)

    barrier = pltpu.get_barrier_semaphore()
    for step in GREET_ROW:
        other = ((place + step) & (ROW - 1))

        @pl.when((other != LATER_DELEGATE) & (other != WIDTH_DELEGATE))
        def _():
            signal(barrier, ctx=row * ROW + other)

    def greet_earlier(r, carry):
        signal(barrier, ctx=r * ROW + LATER_DELEGATE)
        return carry

    lax.fori_loop(0, row, greet_earlier, 0)

    for src, dst, sem in (
        (rate_hbm, poles_v.at[0], poles_sem), (res_hbm, poles_v.at[1], poles_sem),
        (k_hbm, kv_v.at[0], kv_sem), (v_hbm, kv_v.at[1], kv_sem),
        (q_hbm, q_v, q_sem), (gain_hbm, gain_v, gain_sem),
    ):
        pltpu.make_async_copy(src, dst, sem).start()

    for step in range(1, n_ten):
        signal(barrier, ctx=row * ROW + WIDTH_DELEGATE, ten=(ten + step) & (n_ten - 1))

    g_pad[...] = jnp.zeros_like(g_pad)
    wait_bytes(poles_v, poles_sem)
    rate = poles_v[0]
    decay = jnp.exp(-rate)
    decay_sub = jnp.exp(-SUB * rate)
    wait_bytes(kv_v, kv_sem)
    gated = (kv_v[0].astype(F32) * kv_v[1].astype(F32)).astype(jnp.bfloat16).astype(F32)
    g_pad[:, 8:, :] = gated.T.reshape(subs, SUB, chans)

    def advance(i, hs):
        return tuple(decay * h + g_pad[s, pl.ds(8 + i, 1), :] for s, h in enumerate(hs))

    ends = lax.fori_loop(0, SUB, advance, (jnp.zeros((modes, chans), F32),) * subs, unroll=32)
    state = ends[0]
    states[0] = jnp.zeros((modes, chans), F32)
    for s in range(1, subs):
        states[s] = state
        state = decay_sub * state + ends[s]
    decay_all = jnp.exp(-float(tokens) * rate)

    for g in range(groups):
        s_buf[g] = state[:, LANES * g : LANES * (g + 1)]
        a_buf[g] = decay_all[:, LANES * g : LANES * (g + 1)]

    @pl.when(is_plain)
    def _():
        pl.semaphore_wait(barrier, ROW - 1)

    @pl.when(place == WIDTH_DELEGATE ^ 1)
    def _():
        signal(width_in, ctx=row * ROW + WIDTH_DELEGATE)

    @pl.when(place == LATER_DELEGATE ^ 1)
    def _():
        signal(later_in, ctx=row * ROW + LATER_DELEGATE)

    @pl.when(is_width_delegate)
    def _():
        pl.semaphore_wait(width_in, 1)

    @pl.when(is_later_delegate)
    def _():
        pl.semaphore_wait(later_in, 1)

    for step in SEND_ROW:
        other = ((place + step) & (ROW - 1))
        pltpu.make_async_remote_copy(
            s_buf.at[other & (half - 1)], r_buf.at[place], sent_sem, rs1.at[place >> 2], device_id={CTX: row * ROW + other}, device_id_type=MESH
        ).start()

    from_beside = pltpu.make_async_remote_copy(
        s_buf, arrived.at[pl.ds(prefixes, groups)], sent_sem, rs1.at[0], device_id={CTX: me ^ 1}, device_id_type=MESH
    )

    @pl.when(place == 0)
    def _():
        from_beside.start()

    @pl.when(is_later_delegate)
    def _():
        @pl.when(row < n_rows - 1)
        def _():
            pl.semaphore_wait(barrier, ROW * (n_rows - 1 - row))

        for step in SEND_ROW:
            signal(later_in, ctx=row * ROW + ((place + step) & (ROW - 1)))

    weight = poles_v[1] * jnp.sqrt(rate)
    ages = (lax.broadcasted_iota(jnp.int32, (SUB, chans), 0) + 1).astype(F32)
    total = jnp.zeros((SUB, chans), F32)
    for m in range(modes):
        power = weight[m : m + 1, :] * jnp.exp(-rate[m : m + 1, :] * ages)
        powers[m] = power
        total = total + power
    taps[7:8, :] = jnp.sum(weight, axis=0, keepdims=True)
    taps[8:, :] = total
    for s in range(subs):
        decays[s] = jnp.exp(-float(SUB * s) * rate)

    def convolve(k, carry):
        cols = pl.ds(pl.multiple_of(k * LANES, LANES), LANES)
        acc = [jnp.zeros((subs, 8, LANES), F32) for _ in range(SUB // 8)]
        for shift in range(8):
            pieces = [g_pad[:, pl.ds(8 + 8 * j - shift, 8), cols] for j in range(SUB // 8)]
            for b in range(SUB // 8):
                tap = taps[pl.ds(7 + 8 * b + shift, 1), cols]
                for j in range(b, SUB // 8):
                    acc[j] = acc[j] + tap * pieces[j - b]
        for j in range(SUB // 8):
            local[:, pl.ds(8 * j, 8), cols] = acc[j]
        return carry

    lax.fori_loop(0, groups, convolve, 0)

    r_buf[place] = s_buf[mine]

    ratio = a_buf[mine]

    def scan(held, first):
        for d in range(first, first + half):
            p_out[d] = held
            held = ratio * held + r_buf[d]
        return held

    def give_prefixes():
        for step in range(1, half):
            q = (place & half) + ((place + step) & (half - 1))

            @pl.when(q >= 2)
            def _():
                pltpu.make_async_remote_copy(
                    p_out.at[q], arrived.at[prefixes + mine], sent_sem, chip_sem.at[mine >> 1],
                    device_id={CTX: row * ROW + q}, device_id_type=MESH,
                ).start()

    for units, here in ((half - 1 + groups, place == 1), (half - 1, (place < half) & (place != 1)), (half, place >= half)):
        @pl.when(here)
        def _():
            wait_bytes(arrived.at[pl.ds(0, units)], rs1.at[0])

    held = scan(jnp.zeros((modes, LANES), F32), 0)

    @pl.when(place < half)
    def _():
        give_prefixes()
        wait_bytes(arrived.at[pl.ds(0, half)], rs1.at[1])

    @pl.when(place >= half)
    def _():
        wait_bytes(arrived.at[pl.ds(0, half - 1)], rs1.at[1])

    c_out[...] = scan(held, half)

    @pl.when(place >= half)
    def _():
        give_prefixes()

    @pl.when(jnp.logical_not(is_later_delegate))
    def _():
        pl.semaphore_wait(later_in, 1)

    for ahead, chip, core in ORDER:
        @pl.when(row + ahead < n_rows)
        def _():
            pltpu.make_async_remote_copy(
                c_out, arrived.at[groups * row + mine], sent_sem, chip_sem.at[mine >> 1],
                device_id={CTX: (row + ahead) * ROW + (place & half) + 2 * chip + core}, device_id_type=MESH,
            ).start()

    @pl.when(place >= 2)
    def _():
        arrived[prefixes + mine] = p_out[place]

    @pl.when(place == 0)
    def _():
        arrived[prefixes : prefixes + groups] = jnp.zeros((groups, modes, LANES), F32)

    wait_bytes(q_v, q_sem)
    wait_bytes(gain_v, gain_sem)
    q_t[...] = q_v[...].astype(F32).T.reshape(subs, SUB, chans)
    across[...] = jnp.exp(-float(tokens * ROW) * rate)
    before[...] = jnp.exp(-(float(tokens) * place.astype(F32)) * rate)

    @pl.when(is_width_delegate)
    def _():
        pl.semaphore_wait(barrier, ROW * (n_ten - 1))
        for step in SEND_ROW:
            signal(width_in, ctx=row * ROW + ((place + step) & (ROW - 1)))

    def finish(turn, square):
        g = (place & 2) ^ turn
        cols = pl.ds(pl.multiple_of(g * LANES, LANES), LANES)

        count = 2 * row + jnp.where(place < 2, 0, jnp.where(turn < 2, 1, 2))
        for units in range(1, 2 * n_rows + 1):
            @pl.when((count == units) & (turn % 2 == 0))
            def _():
                wait_bytes(arrived.at[pl.ds(0, units)], chip_sem.at[g >> 1])

        def from_row(r, carried):
            return across[:, cols] * carried + arrived[groups * r + g]

        carried = lax.fori_loop(0, row, from_row, jnp.zeros((modes, LANES), F32))
        start = arrived[prefixes + g] + before[:, cols] * carried
        for s in range(subs):
            states[s, :, cols] = states[s, :, cols] + decays[s, :, cols] * start
        acc = local[:, :, cols]
        for m in range(modes):
            acc = acc + powers[m, :, cols][None] * states[:, pl.ds(m, 1), cols]
        out = q_t[:, :, cols] * acc.astype(jnp.bfloat16).astype(F32)
        go_t[:, :, cols] = out * gain_v[:, cols]
        return square + out * out

    square = lax.fori_loop(0, groups, finish, jnp.zeros((subs, SUB, LANES), F32))

    t_buf[ten] = jnp.sum(square.reshape(tokens, LANES).T, axis=0, keepdims=True)

    @pl.when(jnp.logical_not(is_width_delegate))
    def _():
        pl.semaphore_wait(width_in, 1)

    for step in FAR_WIDTH:
        pltpu.make_async_remote_copy(
            t_buf.at[ten], t_buf.at[ten], ss3, rs3,
            device_id={TEN: ((ten + step) & (n_ten - 1))}, device_id_type=MESH,
        ).start()

    go_ref[...] = go_t[...].reshape(tokens, chans).T

    for r in range(n_rows):
        for first, last, prefix_units in ((0, 0, groups + 2), (1, 1, 2), (2, 3, 1), (4, 7, 3)):
            @pl.when((row == r) & (place >= first) & (place <= last))
            def _():
                wait_bytes(arrived.at[pl.ds(0, ROW - 1 + prefix_units + half * (n_rows - 1 - r))], sent_sem)

    wait_bytes(t_buf.at[pl.ds(0, n_ten - 1)], ss3)
    wait_bytes(t_buf.at[pl.ds(0, n_ten - 1)], rs3)
    scale_ref[...] = lax.rsqrt(jnp.sum(t_buf[...], axis=0) / width + 1e-05)


def body(q_gate, k_gate, values, residues, rates, gain):
    n_ctx, n_ten = lax.axis_size(CTX), lax.axis_size(TEN)
    chans, tokens = q_gate.shape
    modes = rates.shape[1]
    subs, groups, n_rows = tokens // SUB, chans // LANES, n_ctx // ROW
    vmem, dma, regular = pltpu.VMEM, pltpu.SemaphoreType.DMA, pltpu.SemaphoreType.REGULAR
    operands = (q_gate, k_gate, values, residues.T, rates.T, gain.reshape(1, chans))
    operands = [pltpu.with_memory_space_constraint(x, pltpu.HBM) for x in operands]
    gated_out, scale = pl.pallas_call(
        functools.partial(kernel, n_ctx, n_ten, float(chans * n_ten)),
        out_shape=(
            vmem((chans, tokens), F32),
            vmem((1, tokens), F32),
        ),
        in_specs=[pl.BlockSpec(memory_space=pltpu.HBM)] * 6,
        out_specs=(pl.BlockSpec(memory_space=pltpu.VMEM), pl.BlockSpec(memory_space=pltpu.VMEM)),
        scratch_shapes=[
            vmem((chans, tokens), jnp.bfloat16),
            vmem((2, chans, tokens), jnp.bfloat16),
            vmem((2, modes, chans), F32),
            vmem((1, chans), F32),
            vmem((subs, SUB, chans), F32),
            vmem((subs, 8 + SUB, chans), F32),
            vmem((8 + SUB, chans), F32),
            vmem((modes, SUB, chans), F32),
            vmem((subs, SUB, chans), F32),
            vmem((subs, SUB, chans), F32),
            vmem((subs, modes, chans), F32),
            vmem((subs, modes, chans), F32),
            vmem((modes, chans), F32),
            vmem((modes, chans), F32),
            vmem((groups, modes, LANES), F32),
            vmem((groups, modes, LANES), F32),
            vmem((ROW, modes, LANES), F32),
            vmem((ROW, modes, LANES), F32),
            vmem((modes, LANES), F32),
            vmem((ROW + groups * (n_rows + 1), modes, LANES), F32),
            vmem((n_ten, 1, tokens), F32),
            dma(()), dma(()), dma(()), dma(()),
            dma((2,)), dma((2,)), dma(()), dma(()), dma(()),
            regular, regular,
        ],
        compiler_params=pltpu.CompilerParams(
            collective_id=0, has_side_effects=True, vmem_limit_bytes=32 * 1024 * 1024
        ),
        name="hyena",
    )(*operands)
    return (gated_out * scale).astype(jnp.bfloat16)


def solution(mesh):
    return jax.shard_map(
        body,
        mesh=mesh,
        in_specs=(
            P(TEN, CTX),
            P(TEN, CTX),
            P(TEN, CTX),
            P(TEN, None),
            P(TEN, None),
            P(TEN),
        ),
        out_specs=P(TEN, CTX),
        check_vma=False,
    )
```
